32 devices in a mesh: sub: 8 (over z, x), coarse: 4 (over y, core).
Axes of the slice: x: 2, y: 2, z: 4, core: 2. Of those that a mesh axis runs over, the one named last changes fastest.
Arguments:
- loads: float32 [8, 4, 16, 16, 128], P('sub', 'coarse'), may hold values from -18 to 18
- mode_x: float32 [8, 4, 16, 16], P('sub', 'coarse'), may hold values from -1 to 2
- mode_y: float32 [8, 4, 16, 16], P('sub', 'coarse'), may hold values from -1 to 2
- mode_z: float32 [8, 4, 128, 128], P('sub', 'coarse'), may hold values from -1 to 2
- eigen: float32 [8, 4, 160], P('sub', 'coarse'), may hold values from 0.1 to 2
- classes: int32 [8, 4, 4, 4, 32], P('sub', 'coarse'), may hold values from 0 to 15
- coefficients: float32 [16], replicated, may hold values from 0.25 to 4
- partner: int32 [8, 4, 4, 2], P('sub', 'coarse'), may hold values from 0 to 7, as said below
- rows: int32 [8, 4, 4, 2048], P('sub', 'coarse'), may hold values from 0 to 32767, as said below
- corner_id: int32 [8, 4, 8], P('sub', 'coarse'), may hold values from 0 to 31, as said below
- corner_row: int32 [8, 4, 8], P('sub', 'coarse'), may hold values from 0 to 32767, as said below
- coarse_inverse: float32 [32, 32], P('coarse'), may hold values from -1 to 3, as said below
Outputs:
- multipliers: float32 [8, 4, 4, 2048], P('sub', 'coarse')
- residual: float32 [8, 4, 4, 2048], P('sub', 'coarse')
The draws below stay inside these ranges and needn't reach their ends.
Inputs may be any that keep to these rules, and one draw needn't show every extreme that they name: partner[i, j, c] differs from (i, j) by one in exactly one index, cyclically; partner[partner[i, j, c], c] = (i, j); the 4 partners of one subdomain are its four cyclic neighbours. `rows`: within one subdomain all 4 x 2048 entries are distinct. `corner_id`: within one subdomain the 8 entries are distinct. `corner_row`: within one subdomain the 8 entries are distinct. `coarse_inverse`: symmetric.
All inputs are finite; a program needn't handle non-finite values.
Results may differ from the reference program's by a relative error of at most 0.0003.
Values sent between devices are 32-bit elements; how exact they have to be, the bound alone decides.
A program may use at most 64 MiB of HBM per device.

```python
import math
import jax
import jax.numpy as jnp
from jax import lax

GX = 16
GY = 16
GZ = 128
M = 2048
NC = 4
NP = 8
NCLASS = 16
ITERS = 2
NCOARSE = 32
N_SUB = 8
N_COARSE = 4


def local_orders(key, salt, count):
    keys = jax.random.split(jax.random.fold_in(key, salt), N_SUB * N_COARSE)
    return jax.vmap(lambda single: jax.random.permutation(single, GX * GY * GZ)[:count])(keys)


def draw_rows(key, part):
    return local_orders(key, 11, NC * M).reshape(N_SUB, N_COARSE, NC, M).astype(jnp.int32)


def draw_corner_row(key, part):
    return local_orders(key, 23, NP).reshape(N_SUB, N_COARSE, NP).astype(jnp.int32)


def draw_corner_id(key, part):
    keys = jax.random.split(jax.random.fold_in(key, 31), N_SUB * N_COARSE)
    picked = jax.vmap(lambda single: jax.random.permutation(single, NCOARSE)[:NP])(keys)
    return picked.reshape(N_SUB, N_COARSE, NP).astype(jnp.int32)


def draw_partner(key, part):
    roles = jax.random.permutation(jax.random.fold_in(key, 3), 4).astype(jnp.int32)
    first = jnp.broadcast_to(jnp.arange(N_SUB, dtype=jnp.int32)[:, None], (N_SUB, N_COARSE))
    second = jnp.broadcast_to(jnp.arange(N_COARSE, dtype=jnp.int32)[None, :], (N_SUB, N_COARSE))
    sub_even = jnp.where(first % 2 == 0, (first + 1) % N_SUB, (first - 1) % N_SUB)
    sub_odd = jnp.where(first % 2 == 0, (first - 1) % N_SUB, (first + 1) % N_SUB)
    col_even = jnp.where(second % 2 == 0, (second + 1) % N_COARSE, (second - 1) % N_COARSE)
    col_odd = jnp.where(second % 2 == 0, (second - 1) % N_COARSE, (second + 1) % N_COARSE)
    sub_table = jnp.stack([sub_even, sub_odd, first, first], axis=-1)
    col_table = jnp.stack([second, second, col_even, col_odd], axis=-1)
    picked_sub = sub_table[:, :, roles]
    picked_col = col_table[:, :, roles]
    return jnp.stack([picked_sub, picked_col], axis=-1).astype(jnp.int32)


def draw_loads(key, part):
    first = jax.random.fold_in(jax.random.fold_in(key, 5), 0)
    ramp = (3.0 ** (jnp.arange(N_SUB, dtype=jnp.float32) / (N_SUB - 1)))[:, None, None, None, None]
    shape = (N_SUB, N_COARSE, GX, GY, GZ)
    values = jnp.clip(jax.random.normal(first, shape, jnp.float32), -6.0, 6.0)
    return (values * ramp).astype(jnp.float32)


def draw_mode(key, salt, order):
    noise = jax.random.uniform(jax.random.fold_in(key, salt), (N_SUB, N_COARSE, order, order), jnp.float32, -1.0, 1.0)
    amplitude = 0.3
    eye = (jnp.arange(order)[:, None] == jnp.arange(order)[None, :]).astype(jnp.float32)
    return (eye[None, None] + amplitude * (3.0 / order) ** 0.5 * noise).astype(jnp.float32)


def draw_mode_x(key, part):
    return draw_mode(key, 41, GX)


def draw_mode_y(key, part):
    return draw_mode(key, 43, GY)


def draw_mode_z(key, part):
    return draw_mode(key, 47, GZ)


def draw_coarse_inverse(key, part):
    first, second = jax.random.split(jax.random.fold_in(key, 9))
    bound = 0.9 / NCOARSE
    off = jax.random.uniform(first, (NCOARSE, NCOARSE), jnp.float32, -bound, bound)
    off = 0.5 * (off + off.T)
    top = 2.0
    diag = jax.random.uniform(second, (NCOARSE,), jnp.float32, 1.0, top)
    eye = jnp.arange(NCOARSE)[:, None] == jnp.arange(NCOARSE)[None, :]
    return jnp.where(eye, diag[:, None], off).astype(jnp.float32)


def touch_ends(entries, key, low, top_value):
    longest = entries.shape.index(max(entries.shape))
    spots = []
    for shift in (0, 1):
        where = [jax.random.randint(jax.random.fold_in(key, axis), (), 0, length) for axis, length in enumerate(entries.shape)]
        where[longest] = (where[longest] + shift) % entries.shape[longest]
        spots.append(tuple(where))
    return entries.at[spots[0]].set(low).at[spots[1]].set(top_value)


def block_scale(own_key, dims, cuts, low, high):
    def one(axis_at, parts):
        steps = jax.random.uniform(jax.random.fold_in(jax.random.fold_in(own_key, 6), axis_at), (parts,), jnp.float32, low / len(cuts), high / len(cuts))
        return jnp.repeat(jnp.exp(steps), dims[axis_at] // parts).reshape((-1,) + (1,) * (len(dims) - axis_at - 1))

    gain = one(*cuts[0])
    for cut in cuts[1:]:
        gain = gain * one(*cut)
    return gain


def setup_inputs(seed: int = 0) -> dict:
    key_of = jax.random.split(jax.random.key(seed), 13)
    loads = draw_loads(jax.random.fold_in(key_of[12], 71), 0)
    mode_x = draw_mode_x(jax.random.fold_in(key_of[12], 71), 0)
    mode_y = draw_mode_y(jax.random.fold_in(key_of[12], 71), 0)
    mode_z = draw_mode_z(jax.random.fold_in(key_of[12], 71), 0)
    eigen = jnp.clip(jnp.exp(math.log(2.0) - 2.9957323 * jax.random.uniform(key_of[4], (N_SUB, N_COARSE, GX + GY + GZ), jnp.float32) ** block_scale(key_of[4], (N_SUB, N_COARSE, GX + GY + GZ), ((0, 8), (1, 4)), -0.2, 0.2)), 0.1, 2.0)
    classes = touch_ends(jax.random.randint(key_of[5], (N_SUB, N_COARSE, GX // 4, GY // 4, GZ // 4), 0, NCLASS), jax.random.fold_in(key_of[5], 1), 0, NCLASS - 1).astype(jnp.int32)
    coefficients = jnp.clip(jnp.exp(jax.random.uniform(key_of[6], (NCLASS,), jnp.float32, math.log(0.25), math.log(4.0))), 0.25, 4.0)
    partner = draw_partner(jax.random.fold_in(key_of[12], 71), 0)
    rows = draw_rows(jax.random.fold_in(key_of[12], 71), 0)
    corner_id = draw_corner_id(jax.random.fold_in(key_of[12], 71), 0)
    corner_row = draw_corner_row(jax.random.fold_in(key_of[12], 71), 0)
    coarse_inverse = draw_coarse_inverse(jax.random.fold_in(key_of[12], 71), 0)
    return {"loads": loads, "mode_x": mode_x, "mode_y": mode_y, "mode_z": mode_z, "eigen": eigen, "classes": classes, "coefficients": coefficients, "partner": partner, "rows": rows, "corner_id": corner_id, "corner_row": corner_row, "coarse_inverse": coarse_inverse}


def fdm_single(args):
    side_x, side_y, side_z, spectrum, root, field = args
    lam_inv = 1.0 / (spectrum[:GX][:, None, None] + spectrum[GX:GX + GY][None, :, None] + spectrum[GX + GY:][None, None, :])
    values = field * root
    values = jnp.einsum('pa,pyz->ayz', side_x, values, precision=lax.Precision.HIGHEST)
    values = jnp.einsum('pb,xpz->xbz', side_y, values, precision=lax.Precision.HIGHEST)
    values = jnp.einsum('xyp,pc->xyc', values, side_z, precision=lax.Precision.HIGHEST)
    values = values * lam_inv
    values = jnp.einsum('ap,pyz->ayz', side_x, values, precision=lax.Precision.HIGHEST)
    values = jnp.einsum('bp,xpz->xbz', side_y, values, precision=lax.Precision.HIGHEST)
    values = jnp.einsum('xyp,cp->xyc', values, side_z, precision=lax.Precision.HIGHEST)
    return values * root

def reference(loads, mode_x, mode_y, mode_z, eigen, classes, coefficients, partner, rows, corner_id, corner_row, coarse_inverse):
    count = N_SUB * N_COARSE
    nodes = GX * GY * GZ
    coef_elem = coefficients[classes]
    coef_node = jnp.repeat(jnp.repeat(jnp.repeat(coef_elem, 4, axis=2), 4, axis=3), 4, axis=4).reshape(count, GX, GY, GZ)
    root = 1.0 / jnp.sqrt(coef_node)
    side_x = mode_x.reshape(count, GX, GX)
    side_y = mode_y.reshape(count, GY, GY)
    side_z = mode_z.reshape(count, GZ, GZ)
    spectra = eigen.reshape(count, GX + GY + GZ)
    sub_index = jnp.arange(N_SUB, dtype=jnp.int32)[:, None, None]
    col_index = jnp.arange(N_COARSE, dtype=jnp.int32)[None, :, None]
    colour_index = jnp.arange(NC, dtype=jnp.int32)[None, None, :]
    mate_sub = partner[..., 0]
    mate_col = partner[..., 1]
    sign = jnp.where(sub_index * N_COARSE + col_index < mate_sub * N_COARSE + mate_col, 1.0, -1.0).astype(jnp.float32)[..., None]
    rows_flat = rows.reshape(count, NC * M)
    dev_index = jnp.arange(count, dtype=jnp.int32)[:, None]
    crow = corner_row.reshape(count, NP)
    cid = corner_id.reshape(count, NP)

    def partner_of(values):
        return values[mate_sub, mate_col, colour_index]

    def at_rows(field):
        return field[dev_index, rows_flat].reshape(N_SUB, N_COARSE, NC, M)

    def jump(field):
        values = at_rows(field)
        return sign * (values - partner_of(values))

    def solve(field):
        shaped = field.reshape(count, GX, GY, GZ)
        return lax.map(fdm_single, (side_x, side_y, side_z, spectra, root, shaped)).reshape(count, nodes)
    a_rows = coef_node.reshape(count, nodes)[dev_index, rows_flat].reshape(N_SUB, N_COARSE, NC, M)
    a_far = partner_of(a_rows)
    weight = a_rows * a_far / (a_rows + a_far)

    def apply_dual(lam):
        source = jnp.zeros((count, nodes), jnp.float32).at[dev_index, rows_flat].set((sign * lam).reshape(count, NC * M))
        local = solve(source)
        partial_corner = local[dev_index, crow]
        total = jnp.zeros((NCOARSE,), jnp.float32).at[cid.reshape(-1)].add(partial_corner.reshape(-1))
        coarse_sol = jnp.dot(coarse_inverse, total, precision=lax.Precision.HIGHEST)
        extra = jnp.zeros((count, nodes), jnp.float32).at[dev_index, crow].set(coarse_sol[cid])
        return jump(local + solve(extra))
    rhs = jump(solve(loads.reshape(count, nodes)))
    multipliers = jnp.zeros_like(rhs)
    residual = rhs
    precond = weight * residual
    direction = precond
    rz_now = jnp.sum(residual * precond)
    for step in range(ITERS):
        image = apply_dual(direction)
        alpha = rz_now / jnp.sum(direction * image)
        multipliers = multipliers + alpha * direction
        residual = residual - alpha * image
        if step + 1 < ITERS:
            precond = weight * residual
            rz_next = jnp.sum(residual * precond)
            direction = precond + rz_next / rz_now * direction
            rz_now = rz_next
    return (multipliers, residual)
```

```python
import functools

import jax
import jax.numpy as jnp
from jax import lax
from jax.experimental import pallas as pl
from jax.experimental.pallas import tpu as pltpu
from jax.sharding import PartitionSpec as P

ITERS = 2
CHUNK = 512
BF = jnp.bfloat16
F32 = jnp.float32
HI = lax.Precision.HIGHEST
MESH = pl.DeviceIdType.MESH


def exact_dot(a, b):
    return jnp.dot(a, b, precision=HI, preferred_element_type=F32)


def halves(x):
    high = x.astype(BF)
    return high, (x - high.astype(F32)).astype(BF)


def iota(shape, dim):
    return lax.broadcasted_iota(jnp.int32, shape, dim)


def each(low, high, body):
    if high - low <= 8:
        for i in range(low, high):
            body(i)
    else:
        lax.fori_loop(low, high, lambda i, c: (body(i), c)[1], 0)


def right_operand(x):
    high, low = halves(x)
    return jnp.concatenate([high, low, high], axis=0)


def left_operand(x):
    high, low = halves(x)
    return jnp.concatenate([high, high, low], axis=1)


def times(x, right):
    return jnp.dot(left_operand(x), right, preferred_element_type=F32)


def kernel(
    n_sub,
    n_col,
    loads,
    mode_x,
    mode_y,
    mode_z,
    eigen,
    classes,
    coefficients,
    partner,
    rows,
    corner_id,
    corner_row,
    cinv,
    out_mult,
    out_resid,
    onehot,
    node_z,
    el_ref,
    pair_f,
    pair_b,
    side_f,
    side_b,
    lam_ref,
    root_ref,
    corner_l,
    pad_ref,
    cfull,
    send_v,
    recv_v,
    vec_sub,
    vec_col,
    mine_col,
    send_sem,
    recv_sem,
    sub_send,
    sub_recv,
    col_send,
    col_recv,
    cinv_send,
    cinv_recv,
):
    me = lax.axis_index("sub")
    col = lax.axis_index("coarse")
    size_x = mode_x.shape[2]
    size_y = mode_y.shape[2]
    size_z = mode_z.shape[2]
    plane = size_x * size_y
    width = rows.shape[3]
    corners = corner_row.shape[2]
    total_corners = cinv.shape[1]
    padded = vec_sub.shape[3]
    z_shift = size_z.bit_length() - 1

    barrier = pltpu.get_barrier_semaphore()

    def greet_sub(s):
        pl.semaphore_signal(
            barrier, inc=1, device_id=(lax.rem(me + s, n_sub), col), device_id_type=MESH
        )

    def greet_col(s):
        pl.semaphore_signal(
            barrier, inc=1, device_id=(me, lax.rem(col + s, n_col)), device_id_type=MESH
        )

    each(1, n_sub, greet_sub)
    each(1, n_col, greet_col)

    spots = (
        (lax.rem(me + 1, n_sub), col),
        (lax.rem(me + n_sub - 1, n_sub), col),
        (me, lax.rem(col + 1, n_col)),
        (me, lax.rem(col + n_col - 1, n_col)),
    )
    opposite = (1, 0, 3, 2)
    signs = [
        jnp.where(me * n_col + col < s * n_col + c, 1.0, -1.0).astype(F32) for s, c in spots
    ]
    match = [
        [
            jnp.where(
                jnp.logical_and(partner[0, 0, k, 0] == s, partner[0, 0, k, 1] == c), 1, 0
            ).astype(jnp.int32)
            for k in range(4)
        ]
        for s, c in spots
    ]

    for d in range(4):
        picked = match[d][0] * rows[0, 0, 0:1, :]
        for k in range(1, 4):
            picked = picked + match[d][k] * rows[0, 0, k : k + 1, :]
        node_z[d] = lax.bitwise_and(picked, size_z - 1)
        above = lax.shift_right_logical(picked, z_shift)
        for at in range(0, width, CHUNK):
            hit = iota((plane, CHUNK), 0) == above[:, at : at + CHUNK]
            onehot[d, :, at : at + CHUNK] = jnp.where(hit, 1.0, 0.0).astype(BF)

    size_bz = classes.shape[4]
    blocks_y = classes.shape[3]
    blocks_x = classes.shape[2]
    el_ref[...] = jnp.zeros_like(el_ref)
    for bx in range(blocks_x):
        ids = classes[0, 0, bx]
        value = jnp.zeros(ids.shape, F32)
        for n in range(coefficients.shape[0]):
            value = jnp.where(ids == n, coefficients[n], value)
        el_ref[bx * blocks_y : (bx + 1) * blocks_y, 0:size_bz] = value
    el_t = el_ref[...].T[:size_bz, : blocks_x * blocks_y]
    plane_at = iota((blocks_x * blocks_y, plane), 1)
    block_at = (plane_at // (4 * size_y)) * blocks_y + (plane_at % size_y) // 4
    spread = jnp.where(iota((blocks_x * blocks_y, plane), 0) == block_at, 1.0, 0.0)
    coef_block = exact_dot(el_t, spread)
    spread_z = jnp.where(
        iota((size_z, size_bz), 0) // 4 == iota((size_z, size_bz), 1), 1.0, 0.0
    )
    root = exact_dot(spread_z, 1.0 / jnp.sqrt(coef_block))
    root_ref[...] = root

    def copy_of(turn, d):
        return pltpu.make_async_remote_copy(
            src_ref=send_v.at[turn, d],
            dst_ref=recv_v.at[turn, opposite[d]],
            send_sem=send_sem.at[turn, d],
            recv_sem=recv_sem.at[turn, opposite[d]],
            device_id=spots[d],
            device_id_type=MESH,
        )

    def gather(turn, field, shift):
        depth = field.shape[0]
        high, low = halves(field)
        stacked = jnp.concatenate([high, low], axis=0)
        for d in range(4):
            for at in range(0, width, CHUNK):
                part = jnp.dot(
                    stacked, onehot[d, :, at : at + CHUNK], preferred_element_type=F32
                )
                part = part[:depth] + part[depth:]
                at_z = lax.shift_right_logical(node_z[d, :, at : at + CHUNK], shift)
                hit = iota((depth, CHUNK), 0) == at_z
                send_v[turn, d, :, at : at + CHUNK] = jnp.sum(
                    jnp.where(hit, part, 0.0), axis=0, keepdims=True
                )
            copy_of(turn, d).start()

    pl.semaphore_wait(barrier, n_sub - 1 + n_col - 1)

    def cinv_copy(s):
        return pltpu.make_async_remote_copy(
            src_ref=cinv,
            dst_ref=cfull.at[col],
            send_sem=cinv_send.at[s],
            recv_sem=cinv_recv.at[s],
            device_id=(me, lax.rem(col + s, n_col)),
            device_id_type=MESH,
        )

    each(1, n_col, lambda s: cinv_copy(s).start())
    cfull[col] = cinv[...]
    gather(0, coef_block, 2)

    def expand(mode, by_row, by_col):
        size = mode.shape[0]
        left = jnp.where(by_row(iota((plane, size), 0)) == iota((plane, size), 1), 1.0, 0.0)
        right = jnp.where(by_col(iota((size, plane), 1)) == iota((size, plane), 0), 1.0, 0.0)
        return exact_dot(exact_dot(left, mode), right)

    pair = expand(mode_x[0, 0], lambda i: i // size_y, lambda i: i // size_y) * expand(
        mode_y[0, 0], lambda i: i % size_y, lambda i: i % size_y
    )
    side = mode_z[0, 0]
    pair_f[...] = right_operand(pair)
    pair_b[...] = right_operand(pair.T)
    side_f[...] = left_operand(side.T)
    side_b[...] = left_operand(side)

    spectrum = eigen[0]
    modes = spectrum.shape[1]
    mode_at = iota((modes, plane), 0)
    to_plane = jnp.logical_or(
        mode_at == iota((modes, plane), 1) // size_y,
        mode_at == size_x + iota((modes, plane), 1) % size_y,
    )
    plane_eigen = exact_dot(
        jnp.broadcast_to(spectrum, (8, modes)), jnp.where(to_plane, 1.0, 0.0)
    )[0:1]
    z_at = iota((size_z, modes), 0) + size_x + size_y == iota((size_z, modes), 1)
    z_eigen = jnp.sum(jnp.where(z_at, spectrum, 0.0), axis=1, keepdims=True)
    lam_ref[...] = 1.0 / (z_eigen + plane_eigen)

    def forward(field):
        mixed = times(field * root_ref[...], pair_f[...])
        return jnp.dot(side_f[...], right_operand(mixed), preferred_element_type=F32)

    def backward(spectral):
        mixed = times(spectral, pair_b[...])
        return root_ref[...] * jnp.dot(
            side_b[...], right_operand(mixed), preferred_element_type=F32
        )

    gather(1, backward(lam_ref[...] * forward(loads[0, 0].reshape(plane, size_z).T)), 0)

    lane_z = iota((corners, size_z), 1)
    lane_p = iota((corners, plane), 1)
    lane_n = iota((corners, padded), 1)
    at_z = jnp.zeros((corners, size_z), jnp.int32)
    at_p = jnp.zeros((corners, plane), jnp.int32)
    at_n = jnp.zeros((corners, padded), jnp.int32)
    for t in range(corners):
        node = corner_row[0, 0, t]
        at_z = jnp.where(iota((corners, size_z), 0) == t, node, at_z)
        at_p = jnp.where(iota((corners, plane), 0) == t, node, at_p)
        at_n = jnp.where(iota((corners, padded), 0) == t, corner_id[0, 0, t], at_n)
    pick_z = jnp.where(lax.bitwise_and(at_z, size_z - 1) == lane_z, 1.0, 0.0)
    pick_p = jnp.where(lax.shift_right_logical(at_p, z_shift) == lane_p, 1.0, 0.0)
    pick_n = jnp.where(at_n == lane_n, 1.0, 0.0)
    corner_root = jnp.sum(exact_dot(pick_z, root) * pick_p, axis=1, keepdims=True)
    corner_z = exact_dot(pick_z, side)
    corner_p = exact_dot(pick_p, pair) * corner_root
    high, low = halves(corner_z)
    pad_ref[...] = jnp.zeros_like(pad_ref)
    pad_ref[0:corners, :] = high.astype(F32)
    pad_ref[corners : 2 * corners, :] = high.astype(F32)
    pad_ref[2 * corners : 3 * corners, :] = low.astype(F32)
    corner_l[...] = pad_ref[...].T.astype(BF)
    corner_z3 = jnp.concatenate([high.astype(F32), high.astype(F32), low.astype(F32)], axis=1)
    corner_z3 = corner_z3.astype(BF)

    def all_sum(turn, vector):
        vec_sub[turn, 0] = vector

        def sub_copy(s):
            return pltpu.make_async_remote_copy(
                src_ref=vec_sub.at[turn, 0],
                dst_ref=vec_sub.at[turn, s],
                send_sem=sub_send.at[turn, s],
                recv_sem=sub_recv.at[turn, s],
                device_id=(lax.rem(me + s, n_sub), col),
                device_id_type=MESH,
            )

        def col_copy(s):
            return pltpu.make_async_remote_copy(
                src_ref=mine_col.at[turn],
                dst_ref=vec_col.at[turn, s],
                send_sem=col_send.at[turn, s],
                recv_sem=col_recv.at[turn, s],
                device_id=(me, lax.rem(col + s, n_col)),
                device_id_type=MESH,
            )

        each(1, n_sub, lambda s: sub_copy(s).start())
        each(1, n_sub, lambda s: sub_copy(s).wait())
        mine = jnp.sum(vec_sub[turn], axis=0)
        mine_col[turn] = mine
        each(1, n_col, lambda s: col_copy(s).start())
        vec_col[turn, 0] = mine
        each(1, n_col, lambda s: col_copy(s).wait())
        return jnp.sum(vec_col[turn], axis=0)

    def receive(turn):
        for d in range(4):
            copy_of(turn, d).wait()

    def jump(turn):
        receive(turn)
        return [signs[d] * (send_v[turn, d] - recv_v[turn, d]) for d in range(4)]

    def scatter(values):
        total = jnp.zeros((2 * size_z, plane), F32)
        for d in range(4):
            scaled = signs[d] * values[d]
            high = scaled.astype(BF).astype(F32)
            low = scaled - high
            for at in range(0, width, CHUNK):
                hit = iota((size_z, CHUNK), 0) == node_z[d, :, at : at + CHUNK]
                stacked = jnp.concatenate(
                    [
                        jnp.where(hit, high[:, at : at + CHUNK], 0.0).astype(BF),
                        jnp.where(hit, low[:, at : at + CHUNK], 0.0).astype(BF),
                    ],
                    axis=0,
                )
                total = total + lax.dot_general(
                    stacked,
                    onehot[d, :, at : at + CHUNK],
                    (((1,), (1,)), ((), ())),
                    preferred_element_type=F32,
                )
        return total[:size_z] + total[size_z:]

    def all_of(x):
        return jnp.sum(jnp.sum(x, axis=0, keepdims=True), axis=1, keepdims=True)

    def dot4(a, b):
        total = a[0] * b[0]
        for d in range(1, 4):
            total = total + a[d] * b[d]
        return jnp.sum(total, axis=1, keepdims=True)

    first_row = iota((corners, padded), 0) == 0

    def apply(turn, values, scalars):
        modal = forward(scatter(values))
        spectral = lam_ref[...] * modal
        energy = all_of(modal * spectral)
        at_corner = jnp.sum(
            jnp.dot(corner_z3, right_operand(spectral), preferred_element_type=F32) * corner_p,
            axis=1,
            keepdims=True,
        )
        vector = pick_n * at_corner
        for n, scalar in enumerate([energy] + scalars):
            here = jnp.logical_and(first_row, lane_n == total_corners + n)
            vector = jnp.where(here, scalar, vector)
        summed = all_sum(turn - 2, vector)
        if turn == 2:
            each(1, n_col, lambda s: cinv_copy(s).wait())
        inverse = cfull[...].reshape(total_corners, total_corners)
        coarse = jnp.sum(exact_dot(summed[:, :total_corners], inverse), axis=0, keepdims=True)
        total = jnp.sum(summed, axis=0, keepdims=True)
        quad = jnp.sum(total[:, :total_corners] * coarse, axis=1, keepdims=True)
        local = jnp.sum(pick_n[:, :total_corners] * coarse, axis=1, keepdims=True)
        high, low = halves(corner_p * local)
        high, low = high.astype(F32), low.astype(F32)
        rest = jnp.zeros((size_z - 3 * corners, plane), F32)
        source = jnp.concatenate([high, low, high, rest], axis=0).astype(BF)
        extra = jnp.dot(corner_l[...], source, preferred_element_type=F32)
        gather(turn, backward(spectral + lam_ref[...] * extra), 0)
        lane = iota((1, padded), 1)
        got = [
            jnp.sum(jnp.where(lane == total_corners + n, total, 0.0), axis=1, keepdims=True)
            for n in range(1 + len(scalars))
        ]
        return 2.0 * (got[0] + quad), got[1:]

    receive(0)
    weight = []
    for d in range(4):
        near, far = send_v[0, d], recv_v[0, d]
        weight.append(near * far / (near + far))
    four = range(4)
    resid = jump(1)
    direction = [weight[d] * resid[d] for d in four]
    image_dot, (rz,) = apply(2, direction, [dot4(resid, direction)])
    alpha = rz / image_dot
    mult = [alpha * direction[d] for d in four]
    image = jump(2)
    for step in range(1, ITERS):
        resid = [resid[d] - alpha * image[d] for d in four]
        precond = [weight[d] * resid[d] for d in four]
        own_dot, (rz_next, cross) = apply(
            2 + step, precond, [dot4(resid, precond), dot4(precond, image)]
        )
        beta = rz_next / rz
        image_dot = own_dot + 2.0 * beta * cross + beta * beta * image_dot
        alpha = rz_next / image_dot
        rz = rz_next
        direction = [precond[d] + beta * direction[d] for d in four]
        mult = [mult[d] + alpha * direction[d] for d in four]
        fresh = jump(2 + step)
        image = [fresh[d] + beta * image[d] for d in four]
    resid = [resid[d] - alpha * image[d] for d in four]
    for k in range(4):
        share = [match[d][k].astype(F32) for d in four]
        one = share[0] * mult[0]
        two = share[0] * resid[0]
        for d in range(1, 4):
            one = one + share[d] * mult[d]
            two = two + share[d] * resid[d]
        out_mult[0, 0, k : k + 1, :] = one
        out_resid[0, 0, k : k + 1, :] = two


def on_device(n_sub, n_col, *args):
    loads, mode_x, mode_y, mode_z, eigen, classes = args[:6]
    rows, cinv = args[8], args[11]
    size_z = mode_z.shape[2]
    plane = mode_x.shape[2] * mode_y.shape[2]
    width = rows.shape[3]
    corners = args[10].shape[2]
    total_corners = cinv.shape[1]
    padded = -(-(total_corners + 3) // 128) * 128
    turns = 2 + ITERS
    vmem = pl.BlockSpec(memory_space=pltpu.VMEM)
    smem = pl.BlockSpec(memory_space=pltpu.SMEM)
    dma = pltpu.SemaphoreType.DMA
    out = jax.ShapeDtypeStruct(rows.shape, F32)
    return pl.pallas_call(
        functools.partial(kernel, n_sub, n_col),
        out_shape=(out, out),
        in_specs=[vmem] * 6 + [smem] * 2 + [vmem] + [smem] * 2 + [vmem],
        out_specs=(vmem, vmem),
        scratch_shapes=[
            pltpu.VMEM((4, plane, width), BF),
            pltpu.VMEM((4, 1, width), jnp.int32),
            pltpu.VMEM((128, 128), F32),
            pltpu.VMEM((3 * plane, plane), BF),
            pltpu.VMEM((3 * plane, plane), BF),
            pltpu.VMEM((size_z, 3 * size_z), BF),
            pltpu.VMEM((size_z, 3 * size_z), BF),
            pltpu.VMEM((size_z, plane), F32),
            pltpu.VMEM((size_z, plane), F32),
            pltpu.VMEM((size_z, size_z), BF),
            pltpu.VMEM((size_z, size_z), F32),
            pltpu.VMEM((n_col,) + cinv.shape, F32),
            pltpu.VMEM((turns, 4, 1, width), F32),
            pltpu.VMEM((turns, 4, 1, width), F32),
            pltpu.VMEM((ITERS, n_sub, corners, padded), F32),
            pltpu.VMEM((ITERS, n_col, corners, padded), F32),
            pltpu.VMEM((ITERS, corners, padded), F32),
            dma((turns, 4)),
            dma((turns, 4)),
            dma((ITERS, n_sub)),
            dma((ITERS, n_sub)),
            dma((ITERS, n_col)),
            dma((ITERS, n_col)),
            dma((n_col,)),
            dma((n_col,)),
        ],
        compiler_params=pltpu.CompilerParams(
            collective_id=0, has_side_effects=True, vmem_limit_bytes=48 * 1024 * 1024
        ),
        name="feti_pcg",
    )(*args)


def solution(mesh):
    placed = (
        P("sub", "coarse", None, None, None),
        P("sub", "coarse", None, None),
        P("sub", "coarse", None, None),
        P("sub", "coarse", None, None),
        P("sub", "coarse", None),
        P("sub", "coarse", None, None, None),
        P(),
        P("sub", "coarse", None, None),
        P("sub", "coarse", None, None),
        P("sub", "coarse", None),
        P("sub", "coarse", None),
        P("coarse", None),
    )
    return jax.shard_map(
        functools.partial(on_device, mesh.shape["sub"], mesh.shape["coarse"]),
        mesh=mesh,
        in_specs=placed,
        out_specs=(P("sub", "coarse", None, None), P("sub", "coarse", None, None)),
        check_vma=False,
    )
```

```python
import functools

import jax
import jax.numpy as jnp
from jax import lax
from jax.experimental import pallas as pl
from jax.experimental.pallas import tpu as pltpu
from jax.sharding import PartitionSpec as P

ITERS = 2
CHUNK = 512
BF = jnp.bfloat16
F32 = jnp.float32
HI = lax.Precision.HIGHEST
MESH = pl.DeviceIdType.MESH


def exact_dot(a, b):
    return jnp.dot(a, b, precision=HI, preferred_element_type=F32)


def halves(x):
    high = x.astype(BF)
    return high, (x - high.astype(F32)).astype(BF)


def iota(shape, dim):
    return lax.broadcasted_iota(jnp.int32, shape, dim)


def each(low, high, body):
    if high - low <= 8:
        for i in range(low, high):
            body(i)
    else:
        lax.fori_loop(low, high, lambda i, c: (body(i), c)[1], 0)


def right_operand(x):
    high, low = halves(x)
    return jnp.concatenate([high, low, high], axis=0)


def left_operand(x):
    high, low = halves(x)
    return jnp.concatenate([high, high, low], axis=1)


def times(x, right):
    return jnp.dot(left_operand(x), right, preferred_element_type=F32)


def kernel(
    n_sub,
    n_col,
    loads_hbm,
    mode_x_hbm,
    mode_y_hbm,
    mode_z_hbm,
    eigen_hbm,
    classes_hbm,
    coefficients,
    partner,
    rows_hbm,
    corner_id,
    corner_row,
    cinv_hbm,
    out_mult,
    out_resid,
    loads,
    mode_x,
    mode_y,
    mode_z,
    eigen,
    classes,
    rows,
    cinv,
    load_sem,
    onehot,
    masks,
    placed_rows,
    node_z,
    el_ref,
    pair_f,
    pair_b,
    side_f,
    side_b,
    lam_ref,
    root_ref,
    corner_l,
    pad_ref,
    cfull,
    send_v,
    recv_v,
    vec_sub,
    vec_col,
    mine_col,
    send_sem,
    recv_sem,
    sub_send,
    sub_recv,
    col_send,
    col_recv,
    cinv_send,
    cinv_recv,
):
    me = lax.axis_index("sub")
    col = lax.axis_index("coarse")
    size_x = mode_x.shape[2]
    size_y = mode_y.shape[2]
    size_z = mode_z.shape[2]
    plane = size_x * size_y
    width = rows.shape[3]
    corners = corner_row.shape[2]
    total_corners = cinv.shape[1]
    padded = vec_sub.shape[3]
    z_shift = size_z.bit_length() - 1
    y_shift = size_y.bit_length() - 1
    assert size_z == 1 << z_shift and size_y == 1 << y_shift

    fetches = [
        pltpu.make_async_copy(source, target, load_sem.at[n])
        for n, (source, target) in enumerate(
            (
                (rows_hbm, rows),
                (classes_hbm, classes),
                (cinv_hbm, cinv),
                (mode_x_hbm, mode_x),
                (mode_y_hbm, mode_y),
                (mode_z_hbm, mode_z),
                (eigen_hbm, eigen),
                (loads_hbm, loads),
            )
        )
    ]
    for fetch in fetches:
        fetch.start()
    barrier = pltpu.get_barrier_semaphore()

    def greet_sub(s):
        pl.semaphore_signal(
            barrier, inc=1, device_id=(lax.rem(me + s, n_sub), col), device_id_type=MESH
        )

    def greet_col(s):
        pl.semaphore_signal(
            barrier, inc=1, device_id=(me, lax.rem(col + s, n_col)), device_id_type=MESH
        )

    each(1, n_sub, greet_sub)
    each(1, n_col, greet_col)

    spots = (
        (lax.rem(me + 1, n_sub), col),
        (lax.rem(me + n_sub - 1, n_sub), col),
        (me, lax.rem(col + 1, n_col)),
        (me, lax.rem(col + n_col - 1, n_col)),
    )
    opposite = (1, 0, 3, 2)
    signs = [
        jnp.where(me * n_col + col < s * n_col + c, 1.0, -1.0).astype(F32) for s, c in spots
    ]
    match = [
        [
            jnp.where(
                jnp.logical_and(partner[0, 0, 0, k] == s, partner[0, 0, 1, k] == c), 1, 0
            ).astype(jnp.int32)
            for k in range(4)
        ]
        for s, c in spots
    ]

    for fetch in fetches:
        fetch.wait()

    for d in range(4):
        picked = match[d][0] * rows[0, 0, 0:1, :]
        for k in range(1, 4):
            picked = picked + match[d][k] * rows[0, 0, k : k + 1, :]
        node_z[d] = lax.bitwise_and(picked, size_z - 1)
        above = lax.shift_right_logical(picked, z_shift)
        for at in range(0, width, CHUNK):
            hit = iota((plane, CHUNK), 0) == above[:, at : at + CHUNK]
            here = slice(d * width + at, d * width + at + CHUNK)
            onehot[:, here] = jnp.where(hit, 1.0, 0.0).astype(BF)
            hit = iota((size_z, CHUNK), 0) == node_z[d, :, at : at + CHUNK]
            masks[:, here] = jnp.where(hit, 1.0, 0.0).astype(BF)

    size_bz = classes.shape[4]
    blocks_y = classes.shape[3]
    blocks_x = classes.shape[2]
    el_ref[...] = jnp.zeros_like(el_ref)
    for bx in range(blocks_x):
        ids = classes[0, 0, bx]
        value = jnp.zeros(ids.shape, F32)
        for n in range(coefficients.shape[0]):
            value = jnp.where(ids == n, coefficients[n], value)
        el_ref[bx * blocks_y : (bx + 1) * blocks_y, 0:size_bz] = value
    el_t = el_ref[...].T[:size_bz, : blocks_x * blocks_y]
    plane_at = iota((blocks_x * blocks_y, plane), 1)
    block_at = lax.shift_right_logical(plane_at, y_shift + 2) * blocks_y
    block_at = block_at + lax.shift_right_logical(lax.bitwise_and(plane_at, size_y - 1), 2)
    spread = jnp.where(iota((blocks_x * blocks_y, plane), 0) == block_at, 1.0, 0.0)
    coef_block = exact_dot(el_t, spread)
    spread_z = jnp.where(
        lax.shift_right_logical(iota((size_z, size_bz), 0), 2) == iota((size_z, size_bz), 1), 1.0, 0.0
    )
    root = exact_dot(spread_z, 1.0 / jnp.sqrt(coef_block))
    root_ref[...] = root

    def copy_of(turn, d):
        return pltpu.make_async_remote_copy(
            src_ref=send_v.at[turn, d],
            dst_ref=recv_v.at[turn, opposite[d]],
            send_sem=send_sem.at[turn, d],
            recv_sem=recv_sem.at[turn, opposite[d]],
            device_id=spots[d],
            device_id_type=MESH,
        )

    def gather(turn, field, shift):
        depth = field.shape[0]
        high, low = halves(field)
        stacked = jnp.concatenate([high, low], axis=0)
        for d in range(4):
            for at in range(0, width, CHUNK):
                part = jnp.dot(
                    stacked,
                    onehot[:, d * width + at : d * width + at + CHUNK],
                    preferred_element_type=F32,
                )
                part = part[:depth] + part[depth:]
                at_z = lax.shift_right_logical(node_z[d, :, at : at + CHUNK], shift)
                hit = iota((depth, CHUNK), 0) == at_z
                send_v[turn, d, :, at : at + CHUNK] = jnp.sum(
                    jnp.where(hit, part, 0.0), axis=0, keepdims=True
                )
        for d in range(4):
            copy_of(turn, d).start()

    pl.semaphore_wait(barrier, n_sub - 1 + n_col - 1)

    def cinv_copy(s):
        return pltpu.make_async_remote_copy(
            src_ref=cinv,
            dst_ref=cfull.at[col],
            send_sem=cinv_send.at[s],
            recv_sem=cinv_recv.at[s],
            device_id=(me, lax.rem(col + s, n_col)),
            device_id_type=MESH,
        )

    each(1, n_col, lambda s: cinv_copy(s).start())
    cfull[col] = cinv[...]
    gather(0, coef_block, 2)

    def of_x(i):
        return lax.shift_right_logical(i, y_shift)

    def of_y(i):
        return lax.bitwise_and(i, size_y - 1)

    def expand(mode, of):
        size = mode.shape[0]
        left = jnp.where(of(iota((plane, size), 0)) == iota((plane, size), 1), 1.0, 0.0)
        right = jnp.where(of(iota((size, plane), 1)) == iota((size, plane), 0), 1.0, 0.0)
        left, right = left.astype(BF), right.astype(BF)
        parts = [
            jnp.dot(
                jnp.dot(left, part, preferred_element_type=F32).astype(BF),
                right,
                preferred_element_type=F32,
            )
            for part in halves(mode)
        ]
        return parts[0] + parts[1]

    pair = expand(mode_x[0, 0], of_x) * expand(mode_y[0, 0], of_y)
    side = mode_z[0, 0]
    pair_f[...] = right_operand(pair)
    pair_b[...] = right_operand(pair.T)
    side_f[...] = left_operand(side.T)
    side_b[...] = left_operand(side)

    spectrum = eigen[0]
    modes = spectrum.shape[1]
    mode_at = iota((modes, plane), 0)
    to_plane = jnp.logical_or(
        mode_at == of_x(iota((modes, plane), 1)),
        mode_at == size_x + of_y(iota((modes, plane), 1)),
    )
    plane_eigen = exact_dot(
        jnp.broadcast_to(spectrum, (8, modes)), jnp.where(to_plane, 1.0, 0.0)
    )[0:1]
    z_at = iota((size_z, modes), 0) + size_x + size_y == iota((size_z, modes), 1)
    z_eigen = jnp.sum(jnp.where(z_at, spectrum, 0.0), axis=1, keepdims=True)
    lam_ref[...] = 1.0 / (z_eigen + plane_eigen)

    def forward(field):
        mixed = times(field * root_ref[...], pair_f[...])
        return jnp.dot(side_f[...], right_operand(mixed), preferred_element_type=F32)

    def backward(spectral):
        mixed = times(spectral, pair_b[...])
        return root_ref[...] * jnp.dot(
            side_b[...], right_operand(mixed), preferred_element_type=F32
        )

    gather(1, backward(lam_ref[...] * forward(loads[0, 0].reshape(plane, size_z).T)), 0)

    lane_z = iota((corners, size_z), 1)
    lane_p = iota((corners, plane), 1)
    lane_n = iota((corners, padded), 1)
    at_z = jnp.zeros((corners, size_z), jnp.int32)
    at_p = jnp.zeros((corners, plane), jnp.int32)
    at_n = jnp.zeros((corners, padded), jnp.int32)
    for t in range(corners):
        node = corner_row[0, 0, t]
        at_z = jnp.where(iota((corners, size_z), 0) == t, node, at_z)
        at_p = jnp.where(iota((corners, plane), 0) == t, node, at_p)
        at_n = jnp.where(iota((corners, padded), 0) == t, corner_id[0, 0, t], at_n)
    pick_z = jnp.where(lax.bitwise_and(at_z, size_z - 1) == lane_z, 1.0, 0.0)
    pick_p = jnp.where(lax.shift_right_logical(at_p, z_shift) == lane_p, 1.0, 0.0)
    pick_n = jnp.where(at_n == lane_n, 1.0, 0.0)
    corner_root = jnp.sum(exact_dot(pick_z, root) * pick_p, axis=1, keepdims=True)
    corner_z = exact_dot(pick_z, side)
    corner_p = exact_dot(pick_p, pair) * corner_root
    high, low = halves(corner_z)
    pad_ref[...] = jnp.zeros_like(pad_ref)
    pad_ref[0:corners, :] = high.astype(F32)
    pad_ref[corners : 2 * corners, :] = high.astype(F32)
    pad_ref[2 * corners : 3 * corners, :] = low.astype(F32)
    corner_l[...] = pad_ref[...].T.astype(BF)
    corner_z3 = jnp.concatenate([high.astype(F32), high.astype(F32), low.astype(F32)], axis=1)
    corner_z3 = corner_z3.astype(BF)

    def all_sum(turn, vector):
        vec_sub[turn, 0] = vector

        def sub_copy(s):
            return pltpu.make_async_remote_copy(
                src_ref=vec_sub.at[turn, 0],
                dst_ref=vec_sub.at[turn, s],
                send_sem=sub_send.at[turn, s],
                recv_sem=sub_recv.at[turn, s],
                device_id=(lax.rem(me + s, n_sub), col),
                device_id_type=MESH,
            )

        def col_copy(s):
            return pltpu.make_async_remote_copy(
                src_ref=mine_col.at[turn],
                dst_ref=vec_col.at[turn, s],
                send_sem=col_send.at[turn, s],
                recv_sem=col_recv.at[turn, s],
                device_id=(me, lax.rem(col + s, n_col)),
                device_id_type=MESH,
            )

        each(1, n_sub, lambda s: sub_copy(s).start())
        each(1, n_sub, lambda s: sub_copy(s).wait())
        mine = jnp.sum(vec_sub[turn], axis=0)
        mine_col[turn] = mine
        each(1, n_col, lambda s: col_copy(s).start())
        vec_col[turn, 0] = mine
        each(1, n_col, lambda s: col_copy(s).wait())
        return jnp.sum(vec_col[turn], axis=0)

    def receive(turn):
        for d in range(4):
            copy_of(turn, d).wait()

    def jump(turn):
        receive(turn)
        return [signs[d] * (send_v[turn, d] - recv_v[turn, d]) for d in range(4)]

    def scatter(values):
        for d in range(4):
            high, low = halves(signs[d] * values[d])
            for at in range(0, width, CHUNK):
                here = slice(d * width + at, d * width + at + CHUNK)
                mask = masks[:, here]
                placed_rows[:size_z, here] = mask * high[:, at : at + CHUNK]
                placed_rows[size_z:, here] = mask * low[:, at : at + CHUNK]
        total = lax.dot_general(
            placed_rows[...],
            onehot[...],
            (((1,), (1,)), ((), ())),
            preferred_element_type=F32,
        )
        return total[:size_z] + total[size_z:]

    def all_of(x):
        return jnp.sum(jnp.sum(x, axis=0, keepdims=True), axis=1, keepdims=True)

    def dot4(a, b):
        total = a[0] * b[0]
        for d in range(1, 4):
            total = total + a[d] * b[d]
        return jnp.sum(total, axis=1, keepdims=True)

    first_row = iota((corners, padded), 0) == 0

    def apply(turn, values, scalars):
        modal = forward(scatter(values))
        spectral = lam_ref[...] * modal
        energy = all_of(modal * spectral)
        at_corner = jnp.sum(
            jnp.dot(corner_z3, right_operand(spectral), preferred_element_type=F32) * corner_p,
            axis=1,
            keepdims=True,
        )
        vector = pick_n * at_corner
        for n, scalar in enumerate([energy] + scalars):
            here = jnp.logical_and(first_row, lane_n == total_corners + n)
            vector = jnp.where(here, scalar, vector)
        summed = all_sum(turn - 2, vector)
        if turn == 2:
            each(1, n_col, lambda s: cinv_copy(s).wait())
        inverse = cfull[...].reshape(total_corners, total_corners)
        coarse = jnp.sum(exact_dot(summed[:, :total_corners], inverse), axis=0, keepdims=True)
        total = jnp.sum(summed, axis=0, keepdims=True)
        quad = jnp.sum(total[:, :total_corners] * coarse, axis=1, keepdims=True)
        local = jnp.sum(pick_n[:, :total_corners] * coarse, axis=1, keepdims=True)
        high, low = halves(corner_p * local)
        high, low = high.astype(F32), low.astype(F32)
        rest = jnp.zeros((size_z - 3 * corners, plane), F32)
        source = jnp.concatenate([high, low, high, rest], axis=0).astype(BF)
        extra = jnp.dot(corner_l[...], source, preferred_element_type=F32)
        gather(turn, backward(spectral + lam_ref[...] * extra), 0)
        lane = iota((1, padded), 1)
        got = [
            jnp.sum(jnp.where(lane == total_corners + n, total, 0.0), axis=1, keepdims=True)
            for n in range(1 + len(scalars))
        ]
        return 2.0 * (got[0] + quad), got[1:]

    receive(0)
    weight = []
    for d in range(4):
        near, far = send_v[0, d], recv_v[0, d]
        weight.append(near * far / (near + far))
    four = range(4)
    resid = jump(1)
    direction = [weight[d] * resid[d] for d in four]
    image_dot, (rz,) = apply(2, direction, [dot4(resid, direction)])
    alpha = rz / image_dot
    mult = [alpha * direction[d] for d in four]
    image = jump(2)
    for step in range(1, ITERS):
        resid = [resid[d] - alpha * image[d] for d in four]
        precond = [weight[d] * resid[d] for d in four]
        own_dot, (rz_next, cross) = apply(
            2 + step, precond, [dot4(resid, precond), dot4(precond, image)]
        )
        beta = rz_next / rz
        image_dot = own_dot + 2.0 * beta * cross + beta * beta * image_dot
        alpha = rz_next / image_dot
        rz = rz_next
        direction = [precond[d] + beta * direction[d] for d in four]
        mult = [mult[d] + alpha * direction[d] for d in four]
        fresh = jump(2 + step)
        image = [fresh[d] + beta * image[d] for d in four]
    resid = [resid[d] - alpha * image[d] for d in four]
    for k in range(4):
        share = [match[d][k].astype(F32) for d in four]
        one = share[0] * mult[0]
        two = share[0] * resid[0]
        for d in range(1, 4):
            one = one + share[d] * mult[d]
            two = two + share[d] * resid[d]
        out_mult[0, 0, k : k + 1, :] = one
        out_resid[0, 0, k : k + 1, :] = two


def on_device(n_sub, n_col, *args):
    args = list(args)
    args[7] = jnp.swapaxes(args[7], 2, 3)
    loads, mode_x, mode_y, mode_z, eigen, classes = args[:6]
    rows, cinv = args[8], args[11]
    size_z = mode_z.shape[2]
    plane = mode_x.shape[2] * mode_y.shape[2]
    width = rows.shape[3]
    corners = args[10].shape[2]
    total_corners = cinv.shape[1]
    padded = -(-(total_corners + 3) // 128) * 128
    turns = 2 + ITERS
    vmem = pl.BlockSpec(memory_space=pltpu.VMEM)
    hbm = pl.BlockSpec(memory_space=pltpu.HBM)
    smem = pl.BlockSpec(memory_space=pltpu.SMEM)
    dma = pltpu.SemaphoreType.DMA
    out = jax.ShapeDtypeStruct(rows.shape, F32)
    return pl.pallas_call(
        functools.partial(kernel, n_sub, n_col),
        out_shape=(out, out),
        in_specs=[hbm] * 6 + [smem] * 2 + [hbm] + [smem] * 2 + [hbm],
        out_specs=(vmem, vmem),
        scratch_shapes=[
            *[
                pltpu.VMEM(x.shape, x.dtype)
                for x in (loads, mode_x, mode_y, mode_z, eigen, classes, rows, cinv)
            ],
            dma((8,)),
            pltpu.VMEM((plane, 4 * width), BF),
            pltpu.VMEM((size_z, 4 * width), BF),
            pltpu.VMEM((2 * size_z, 4 * width), BF),
            pltpu.VMEM((4, 1, width), jnp.int32),
            pltpu.VMEM((128, 128), F32),
            pltpu.VMEM((3 * plane, plane), BF),
            pltpu.VMEM((3 * plane, plane), BF),
            pltpu.VMEM((size_z, 3 * size_z), BF),
            pltpu.VMEM((size_z, 3 * size_z), BF),
            pltpu.VMEM((size_z, plane), F32),
            pltpu.VMEM((size_z, plane), F32),
            pltpu.VMEM((size_z, size_z), BF),
            pltpu.VMEM((size_z, size_z), F32),
            pltpu.VMEM((n_col,) + cinv.shape, F32),
            pltpu.VMEM((turns, 4, 1, width), F32),
            pltpu.VMEM((turns, 4, 1, width), F32),
            pltpu.VMEM((ITERS, n_sub, corners, padded), F32),
            pltpu.VMEM((ITERS, n_col, corners, padded), F32),
            pltpu.VMEM((ITERS, corners, padded), F32),
            dma((turns, 4)),
            dma((turns, 4)),
            dma((ITERS, n_sub)),
            dma((ITERS, n_sub)),
            dma((ITERS, n_col)),
            dma((ITERS, n_col)),
            dma((n_col,)),
            dma((n_col,)),
        ],
        compiler_params=pltpu.CompilerParams(
            collective_id=0, has_side_effects=True, vmem_limit_bytes=48 * 1024 * 1024
        ),
        name="feti_pcg",
    )(*args)


def solution(mesh):
    placed = (
        P("sub", "coarse", None, None, None),
        P("sub", "coarse", None, None),
        P("sub", "coarse", None, None),
        P("sub", "coarse", None, None),
        P("sub", "coarse", None),
        P("sub", "coarse", None, None, None),
        P(),
        P("sub", "coarse", None, None),
        P("sub", "coarse", None, None),
        P("sub", "coarse", None),
        P("sub", "coarse", None),
        P("coarse", None),
    )
    return jax.shard_map(
        functools.partial(on_device, mesh.shape["sub"], mesh.shape["coarse"]),
        mesh=mesh,
        in_specs=placed,
        out_specs=(P("sub", "coarse", None, None), P("sub", "coarse", None, None)),
        check_vma=False,
    )
```

```python
import functools

import jax
import jax.numpy as jnp
from jax import lax
from jax.experimental import pallas as pl
from jax.experimental.pallas import tpu as pltpu
from jax.sharding import PartitionSpec as P

ITERS = 2
CHUNK = 512
BF = jnp.bfloat16
F32 = jnp.float32
HI = lax.Precision.HIGHEST
MESH = pl.DeviceIdType.MESH


def exact_dot(a, b):
    return jnp.dot(a, b, precision=HI, preferred_element_type=F32)


def halves(x):
    high = x.astype(BF)
    return high, (x - high.astype(F32)).astype(BF)


def iota(shape, dim):
    return lax.broadcasted_iota(jnp.int32, shape, dim)


def each(low, high, body):
    if high - low <= 8:
        for i in range(low, high):
            body(i)
    else:
        lax.fori_loop(low, high, lambda i, c: (body(i), c)[1], 0)


def right_operand(x):
    high, low = halves(x)
    return jnp.concatenate([high, low, high], axis=0)


def left_operand(x):
    high, low = halves(x)
    return jnp.concatenate([high, high, low], axis=1)


def times(x, right):
    return jnp.dot(left_operand(x), right, preferred_element_type=F32)


def kernel(
    n_sub,
    n_col,
    loads_hbm,
    mode_x_hbm,
    mode_y_hbm,
    mode_z_hbm,
    eigen_hbm,
    classes_hbm,
    coefficients,
    partner,
    rows_hbm,
    corner_id,
    corner_row,
    cinv_hbm,
    out_mult,
    out_resid,
    loads,
    mode_x,
    mode_y,
    mode_z,
    eigen,
    classes,
    rows,
    cinv,
    load_sem,
    onehot,
    masks,
    placed_rows,
    node_z,
    el_ref,
    pair_f,
    pair_b,
    side_f,
    side_b,
    lam_ref,
    root_ref,
    corner_l,
    pad_ref,
    cfull,
    send_v,
    recv_v,
    vec_sub,
    vec_col,
    mine_col,
    send_sem,
    recv_sem,
    sub_send,
    sub_recv,
    col_send,
    col_recv,
    cinv_send,
    cinv_recv,
):
    me = lax.axis_index("sub")
    col = lax.axis_index("coarse")
    size_x = mode_x.shape[2]
    size_y = mode_y.shape[2]
    size_z = mode_z.shape[2]
    plane = size_x * size_y
    width = rows.shape[3]
    corners = corner_row.shape[2]
    total_corners = cinv.shape[1]
    padded = vec_sub.shape[3]
    z_shift = size_z.bit_length() - 1
    y_shift = size_y.bit_length() - 1
    assert size_z == 1 << z_shift and size_y == 1 << y_shift

    fetches = [
        pltpu.make_async_copy(source, target, load_sem.at[n])
        for n, (source, target) in enumerate(
            (
                (rows_hbm, rows),
                (classes_hbm, classes),
                (cinv_hbm, cinv),
                (mode_x_hbm, mode_x),
                (mode_y_hbm, mode_y),
                (mode_z_hbm, mode_z),
                (eigen_hbm, eigen),
                (loads_hbm, loads),
            )
        )
    ]
    for fetch in fetches:
        fetch.start()
    barrier = pltpu.get_barrier_semaphore()

    def greet_sub(s):
        pl.semaphore_signal(
            barrier, inc=1, device_id=(lax.rem(me + s, n_sub), col), device_id_type=MESH
        )

    def greet_col(s):
        pl.semaphore_signal(
            barrier, inc=1, device_id=(me, lax.rem(col + s, n_col)), device_id_type=MESH
        )

    each(1, n_sub, greet_sub)
    each(1, n_col, greet_col)

    spots = (
        (lax.rem(me + 1, n_sub), col),
        (lax.rem(me + n_sub - 1, n_sub), col),
        (me, lax.rem(col + 1, n_col)),
        (me, lax.rem(col + n_col - 1, n_col)),
    )
    opposite = (1, 0, 3, 2)
    signs = [
        jnp.where(me * n_col + col < s * n_col + c, 1.0, -1.0).astype(F32) for s, c in spots
    ]
    match = [
        [
            jnp.where(
                jnp.logical_and(partner[0, 0, 0, k] == s, partner[0, 0, 1, k] == c), 1, 0
            ).astype(jnp.int32)
            for k in range(4)
        ]
        for s, c in spots
    ]

    fetches[0].wait()

    for d in range(4):
        picked = match[d][0] * rows[0, 0, 0:1, :]
        for k in range(1, 4):
            picked = picked + match[d][k] * rows[0, 0, k : k + 1, :]
        node_z[d] = lax.bitwise_and(picked, size_z - 1)
        above = lax.shift_right_logical(picked, z_shift)
        for at in range(0, width, CHUNK):
            hit = iota((plane, CHUNK), 0) == above[:, at : at + CHUNK]
            here = slice(d * width + at, d * width + at + CHUNK)
            onehot[:, here] = jnp.where(hit, 1.0, 0.0).astype(BF)

    size_bz = classes.shape[4]
    blocks_y = classes.shape[3]
    blocks_x = classes.shape[2]
    for fetch in fetches[1:]:
        fetch.wait()
    el_ref[...] = jnp.zeros_like(el_ref)
    for bx in range(blocks_x):
        ids = classes[0, 0, bx]
        value = jnp.zeros(ids.shape, F32)
        for n in range(coefficients.shape[0]):
            value = jnp.where(ids == n, coefficients[n], value)
        el_ref[bx * blocks_y : (bx + 1) * blocks_y, 0:size_bz] = value
    el_t = el_ref[...].T[:size_bz, : blocks_x * blocks_y]
    plane_at = iota((blocks_x * blocks_y, plane), 1)
    block_at = lax.shift_right_logical(plane_at, y_shift + 2) * blocks_y
    block_at = block_at + lax.shift_right_logical(lax.bitwise_and(plane_at, size_y - 1), 2)
    spread = jnp.where(iota((blocks_x * blocks_y, plane), 0) == block_at, 1.0, 0.0)
    coef_block = exact_dot(el_t, spread)
    spread_z = jnp.where(
        lax.shift_right_logical(iota((size_z, size_bz), 0), 2) == iota((size_z, size_bz), 1), 1.0, 0.0
    )
    root = exact_dot(spread_z, 1.0 / jnp.sqrt(coef_block))
    root_ref[...] = root

    def copy_of(turn, d):
        return pltpu.make_async_remote_copy(
            src_ref=send_v.at[turn, d],
            dst_ref=recv_v.at[turn, opposite[d]],
            send_sem=send_sem.at[turn, d],
            recv_sem=recv_sem.at[turn, opposite[d]],
            device_id=spots[d],
            device_id_type=MESH,
        )

    def gather(fields):
        stacked = [half for _, field, _ in fields for half in halves(field)]
        stacked = jnp.concatenate(stacked, axis=0)
        for d in range(4):
            for at in range(0, width, CHUNK):
                part = jnp.dot(
                    stacked,
                    onehot[:, d * width + at : d * width + at + CHUNK],
                    preferred_element_type=F32,
                )
                first = 0
                for turn, field, shift in fields:
                    depth = field.shape[0]
                    both = part[first : first + depth]
                    both = both + part[first + depth : first + 2 * depth]
                    first += 2 * depth
                    at_z = lax.shift_right_logical(node_z[d, :, at : at + CHUNK], shift)
                    hit = iota((depth, CHUNK), 0) == at_z
                    send_v[turn, d, :, at : at + CHUNK] = jnp.sum(
                        jnp.where(hit, both, 0.0), axis=0, keepdims=True
                    )
            for turn, _, _ in fields:
                copy_of(turn, d).start()

    def of_x(i):
        return lax.shift_right_logical(i, y_shift)

    def of_y(i):
        return lax.bitwise_and(i, size_y - 1)

    def expand(mode, of):
        size = mode.shape[0]
        left = jnp.where(of(iota((plane, size), 0)) == iota((plane, size), 1), 1.0, 0.0)
        right = jnp.where(of(iota((size, plane), 1)) == iota((size, plane), 0), 1.0, 0.0)
        left, right = left.astype(BF), right.astype(BF)
        parts = [
            jnp.dot(
                jnp.dot(left, part, preferred_element_type=F32).astype(BF),
                right,
                preferred_element_type=F32,
            )
            for part in halves(mode)
        ]
        return parts[0] + parts[1]

    pair = expand(mode_x[0, 0], of_x) * expand(mode_y[0, 0], of_y)
    side = mode_z[0, 0]
    pair_f[...] = right_operand(pair)
    pair_b[...] = right_operand(pair.T)
    side_f[...] = left_operand(side.T)
    side_b[...] = left_operand(side)

    spectrum = eigen[0]
    modes = spectrum.shape[1]
    mode_at = iota((modes, plane), 0)
    to_plane = jnp.logical_or(
        mode_at == of_x(iota((modes, plane), 1)),
        mode_at == size_x + of_y(iota((modes, plane), 1)),
    )
    plane_eigen = exact_dot(
        jnp.broadcast_to(spectrum, (8, modes)), jnp.where(to_plane, 1.0, 0.0)
    )[0:1]
    z_at = iota((size_z, modes), 0) + size_x + size_y == iota((size_z, modes), 1)
    z_eigen = jnp.sum(jnp.where(z_at, spectrum, 0.0), axis=1, keepdims=True)
    lam_ref[...] = 1.0 / (z_eigen + plane_eigen)

    def forward(field):
        mixed = times(field * root_ref[...], pair_f[...])
        return jnp.dot(side_f[...], right_operand(mixed), preferred_element_type=F32)

    def backward(spectral):
        mixed = times(spectral, pair_b[...])
        return root_ref[...] * jnp.dot(
            side_b[...], right_operand(mixed), preferred_element_type=F32
        )

    load_field = backward(lam_ref[...] * forward(loads[0, 0].reshape(plane, size_z).T))
    pl.semaphore_wait(barrier, n_sub - 1 + n_col - 1)

    def cinv_copy(s):
        return pltpu.make_async_remote_copy(
            src_ref=cinv,
            dst_ref=cfull.at[col],
            send_sem=cinv_send.at[s],
            recv_sem=cinv_recv.at[s],
            device_id=(me, lax.rem(col + s, n_col)),
            device_id_type=MESH,
        )

    each(1, n_col, lambda s: cinv_copy(s).start())
    cfull[col] = cinv[...]
    gather([(0, coef_block, 2), (1, load_field, 0)])
    for d in range(4):
        for at in range(0, width, CHUNK):
            hit = iota((size_z, CHUNK), 0) == node_z[d, :, at : at + CHUNK]
            here = slice(d * width + at, d * width + at + CHUNK)
            masks[:, here] = jnp.where(hit, 1.0, 0.0).astype(BF)

    lane_z = iota((corners, size_z), 1)
    lane_p = iota((corners, plane), 1)
    lane_n = iota((corners, padded), 1)
    at_z = jnp.zeros((corners, size_z), jnp.int32)
    at_p = jnp.zeros((corners, plane), jnp.int32)
    at_n = jnp.zeros((corners, padded), jnp.int32)
    for t in range(corners):
        node = corner_row[0, 0, t]
        at_z = jnp.where(iota((corners, size_z), 0) == t, node, at_z)
        at_p = jnp.where(iota((corners, plane), 0) == t, node, at_p)
        at_n = jnp.where(iota((corners, padded), 0) == t, corner_id[0, 0, t], at_n)
    pick_z = jnp.where(lax.bitwise_and(at_z, size_z - 1) == lane_z, 1.0, 0.0)
    pick_p = jnp.where(lax.shift_right_logical(at_p, z_shift) == lane_p, 1.0, 0.0)
    pick_n = jnp.where(at_n == lane_n, 1.0, 0.0)
    corner_root = jnp.sum(exact_dot(pick_z, root) * pick_p, axis=1, keepdims=True)
    corner_z = exact_dot(pick_z, side)
    corner_p = exact_dot(pick_p, pair) * corner_root
    high, low = halves(corner_z)
    pad_ref[...] = jnp.zeros_like(pad_ref)
    pad_ref[0:corners, :] = high.astype(F32)
    pad_ref[corners : 2 * corners, :] = high.astype(F32)
    pad_ref[2 * corners : 3 * corners, :] = low.astype(F32)
    corner_l[...] = pad_ref[...].T.astype(BF)
    corner_z3 = jnp.concatenate([high.astype(F32), high.astype(F32), low.astype(F32)], axis=1)
    corner_z3 = corner_z3.astype(BF)

    def all_sum(turn, vector):
        vec_sub[turn, 0] = vector

        def sub_copy(s):
            return pltpu.make_async_remote_copy(
                src_ref=vec_sub.at[turn, 0],
                dst_ref=vec_sub.at[turn, s],
                send_sem=sub_send.at[turn, s],
                recv_sem=sub_recv.at[turn, s],
                device_id=(lax.rem(me + s, n_sub), col),
                device_id_type=MESH,
            )

        def col_copy(s):
            return pltpu.make_async_remote_copy(
                src_ref=mine_col.at[turn],
                dst_ref=vec_col.at[turn, s],
                send_sem=col_send.at[turn, s],
                recv_sem=col_recv.at[turn, s],
                device_id=(me, lax.rem(col + s, n_col)),
                device_id_type=MESH,
            )

        each(1, n_sub, lambda s: sub_copy(s).start())
        each(1, n_sub, lambda s: sub_copy(s).wait())
        mine = jnp.sum(vec_sub[turn], axis=0)
        mine_col[turn] = mine
        each(1, n_col, lambda s: col_copy(s).start())
        vec_col[turn, 0] = mine
        each(1, n_col, lambda s: col_copy(s).wait())
        return jnp.sum(vec_col[turn], axis=0)

    def receive(turn):
        for d in range(4):
            copy_of(turn, d).wait()

    def jump(turn):
        receive(turn)
        return [signs[d] * (send_v[turn, d] - recv_v[turn, d]) for d in range(4)]

    def scatter(values):
        for d in range(4):
            high, low = halves(signs[d] * values[d])
            for at in range(0, width, CHUNK):
                here = slice(d * width + at, d * width + at + CHUNK)
                mask = masks[:, here]
                placed_rows[:size_z, here] = mask * high[:, at : at + CHUNK]
                placed_rows[size_z:, here] = mask * low[:, at : at + CHUNK]
        total = lax.dot_general(
            placed_rows[...],
            onehot[...],
            (((1,), (1,)), ((), ())),
            preferred_element_type=F32,
        )
        return total[:size_z] + total[size_z:]

    def all_of(x):
        return jnp.sum(jnp.sum(x, axis=0, keepdims=True), axis=1, keepdims=True)

    def dot4(a, b):
        total = a[0] * b[0]
        for d in range(1, 4):
            total = total + a[d] * b[d]
        return jnp.sum(total, axis=1, keepdims=True)

    first_row = iota((corners, padded), 0) == 0

    def apply(turn, values, scalars):
        modal = forward(scatter(values))
        spectral = lam_ref[...] * modal
        energy = all_of(modal * spectral)
        at_corner = jnp.sum(
            jnp.dot(corner_z3, right_operand(spectral), preferred_element_type=F32) * corner_p,
            axis=1,
            keepdims=True,
        )
        vector = pick_n * at_corner
        for n, scalar in enumerate([energy] + scalars):
            here = jnp.logical_and(first_row, lane_n == total_corners + n)
            vector = jnp.where(here, scalar, vector)
        summed = all_sum(turn - 2, vector)
        if turn == 2:
            each(1, n_col, lambda s: cinv_copy(s).wait())
        inverse = cfull[...].reshape(total_corners, total_corners)
        coarse = jnp.sum(exact_dot(summed[:, :total_corners], inverse), axis=0, keepdims=True)
        total = jnp.sum(summed, axis=0, keepdims=True)
        quad = jnp.sum(total[:, :total_corners] * coarse, axis=1, keepdims=True)
        local = jnp.sum(pick_n[:, :total_corners] * coarse, axis=1, keepdims=True)
        high, low = halves(corner_p * local)
        high, low = high.astype(F32), low.astype(F32)
        rest = jnp.zeros((size_z - 3 * corners, plane), F32)
        source = jnp.concatenate([high, low, high, rest], axis=0).astype(BF)
        extra = jnp.dot(corner_l[...], source, preferred_element_type=F32)
        gather([(turn, backward(spectral + lam_ref[...] * extra), 0)])
        lane = iota((1, padded), 1)
        got = [
            jnp.sum(jnp.where(lane == total_corners + n, total, 0.0), axis=1, keepdims=True)
            for n in range(1 + len(scalars))
        ]
        return 2.0 * (got[0] + quad), got[1:]

    receive(0)
    weight = []
    for d in range(4):
        near, far = send_v[0, d], recv_v[0, d]
        weight.append(near * far / (near + far))
    four = range(4)
    resid = jump(1)
    direction = [weight[d] * resid[d] for d in four]
    image_dot, (rz,) = apply(2, direction, [dot4(resid, direction)])
    alpha = rz / image_dot
    mult = [alpha * direction[d] for d in four]
    image = jump(2)
    for step in range(1, ITERS):
        resid = [resid[d] - alpha * image[d] for d in four]
        precond = [weight[d] * resid[d] for d in four]
        own_dot, (rz_next, cross) = apply(
            2 + step, precond, [dot4(resid, precond), dot4(precond, image)]
        )
        beta = rz_next / rz
        image_dot = own_dot + 2.0 * beta * cross + beta * beta * image_dot
        alpha = rz_next / image_dot
        rz = rz_next
        direction = [precond[d] + beta * direction[d] for d in four]
        mult = [mult[d] + alpha * direction[d] for d in four]
        fresh = jump(2 + step)
        image = [fresh[d] + beta * image[d] for d in four]
    resid = [resid[d] - alpha * image[d] for d in four]
    for k in range(4):
        share = [match[d][k].astype(F32) for d in four]
        one = share[0] * mult[0]
        two = share[0] * resid[0]
        for d in range(1, 4):
            one = one + share[d] * mult[d]
            two = two + share[d] * resid[d]
        out_mult[0, 0, k : k + 1, :] = one
        out_resid[0, 0, k : k + 1, :] = two


def on_device(n_sub, n_col, *args):
    args = list(args)
    args[7] = jnp.swapaxes(args[7], 2, 3)
    loads, mode_x, mode_y, mode_z, eigen, classes = args[:6]
    rows, cinv = args[8], args[11]
    size_z = mode_z.shape[2]
    plane = mode_x.shape[2] * mode_y.shape[2]
    width = rows.shape[3]
    corners = args[10].shape[2]
    total_corners = cinv.shape[1]
    padded = -(-(total_corners + 3) // 128) * 128
    turns = 2 + ITERS
    vmem = pl.BlockSpec(memory_space=pltpu.VMEM)
    hbm = pl.BlockSpec(memory_space=pltpu.HBM)
    smem = pl.BlockSpec(memory_space=pltpu.SMEM)
    dma = pltpu.SemaphoreType.DMA
    out = jax.ShapeDtypeStruct(rows.shape, F32)
    return pl.pallas_call(
        functools.partial(kernel, n_sub, n_col),
        out_shape=(out, out),
        in_specs=[hbm] * 6 + [smem] * 2 + [hbm] + [smem] * 2 + [hbm],
        out_specs=(vmem, vmem),
        scratch_shapes=[
            *[
                pltpu.VMEM(x.shape, x.dtype)
                for x in (loads, mode_x, mode_y, mode_z, eigen, classes, rows, cinv)
            ],
            dma((8,)),
            pltpu.VMEM((plane, 4 * width), BF),
            pltpu.VMEM((size_z, 4 * width), BF),
            pltpu.VMEM((2 * size_z, 4 * width), BF),
            pltpu.VMEM((4, 1, width), jnp.int32),
            pltpu.VMEM((128, 128), F32),
            pltpu.VMEM((3 * plane, plane), BF),
            pltpu.VMEM((3 * plane, plane), BF),
            pltpu.VMEM((size_z, 3 * size_z), BF),
            pltpu.VMEM((size_z, 3 * size_z), BF),
            pltpu.VMEM((size_z, plane), F32),
            pltpu.VMEM((size_z, plane), F32),
            pltpu.VMEM((size_z, size_z), BF),
            pltpu.VMEM((size_z, size_z), F32),
            pltpu.VMEM((n_col,) + cinv.shape, F32),
            pltpu.VMEM((turns, 4, 1, width), F32),
            pltpu.VMEM((turns, 4, 1, width), F32),
            pltpu.VMEM((ITERS, n_sub, corners, padded), F32),
            pltpu.VMEM((ITERS, n_col, corners, padded), F32),
            pltpu.VMEM((ITERS, corners, padded), F32),
            dma((turns, 4)),
            dma((turns, 4)),
            dma((ITERS, n_sub)),
            dma((ITERS, n_sub)),
            dma((ITERS, n_col)),
            dma((ITERS, n_col)),
            dma((n_col,)),
            dma((n_col,)),
        ],
        compiler_params=pltpu.CompilerParams(
            collective_id=0, has_side_effects=True, vmem_limit_bytes=60 * 1024 * 1024
        ),
        name="feti_pcg",
    )(*args)


def solution(mesh):
    placed = (
        P("sub", "coarse", None, None, None),
        P("sub", "coarse", None, None),
        P("sub", "coarse", None, None),
        P("sub", "coarse", None, None),
        P("sub", "coarse", None),
        P("sub", "coarse", None, None, None),
        P(),
        P("sub", "coarse", None, None),
        P("sub", "coarse", None, None),
        P("sub", "coarse", None),
        P("sub", "coarse", None),
        P("coarse", None),
    )
    return jax.shard_map(
        functools.partial(on_device, mesh.shape["sub"], mesh.shape["coarse"]),
        mesh=mesh,
        in_specs=placed,
        out_specs=(P("sub", "coarse", None, None), P("sub", "coarse", None, None)),
        check_vma=False,
    )
```

```python
import functools

import jax
import jax.numpy as jnp
from jax import lax
from jax.experimental import pallas as pl
from jax.experimental.pallas import tpu as pltpu
from jax.sharding import PartitionSpec as P

ITERS = 2
CHUNK = 512
BF = jnp.bfloat16
F32 = jnp.float32
HI = lax.Precision.HIGHEST
MESH = pl.DeviceIdType.MESH


def exact_dot(a, b):
    return jnp.dot(a, b, precision=HI, preferred_element_type=F32)


def halves(x):
    high = x.astype(BF)
    return high, (x - high.astype(F32)).astype(BF)


def iota(shape, dim):
    return lax.broadcasted_iota(jnp.int32, shape, dim)


def each(low, high, body):
    if high - low <= 8:
        for i in range(low, high):
            body(i)
    else:
        lax.fori_loop(low, high, lambda i, c: (body(i), c)[1], 0)


def right_operand(x):
    high, low = halves(x)
    return jnp.concatenate([high, low, high], axis=0)


def left_operand(x):
    high, low = halves(x)
    return jnp.concatenate([high, high, low], axis=1)


def times(x, right):
    return jnp.dot(left_operand(x), right, preferred_element_type=F32)


def kernel(
    n_sub,
    n_col,
    loads_hbm,
    mode_x_hbm,
    mode_y_hbm,
    mode_z_hbm,
    eigen_hbm,
    classes_hbm,
    coefficients,
    partner,
    rows_hbm,
    corner_id,
    corner_row,
    cinv_hbm,
    out_mult,
    out_resid,
    loads,
    mode_x,
    mode_y,
    mode_z,
    eigen,
    classes,
    rows,
    cinv,
    load_sem,
    onehot,
    masks,
    placed_rows,
    node_z,
    node_p,
    scaled,
    el_ref,
    pair_f,
    pair_b,
    side_f,
    side_b,
    lam_ref,
    root_ref,
    corner_l,
    pad_ref,
    cfull,
    send_v,
    recv_v,
    vec_sub,
    vec_col,
    mine_col,
    send_sem,
    recv_sem,
    sub_send,
    sub_recv,
    col_send,
    col_recv,
    cinv_send,
    cinv_recv,
):
    me = lax.axis_index("sub")
    col = lax.axis_index("coarse")
    size_x = mode_x.shape[2]
    size_y = mode_y.shape[2]
    size_z = mode_z.shape[2]
    plane = size_x * size_y
    width = rows.shape[3]
    corners = corner_row.shape[2]
    total_corners = cinv.shape[1]
    padded = vec_sub.shape[3]
    z_shift = size_z.bit_length() - 1
    y_shift = size_y.bit_length() - 1
    assert size_z == 1 << z_shift and size_y == 1 << y_shift

    fetches = [
        pltpu.make_async_copy(source, target, load_sem.at[n])
        for n, (source, target) in enumerate(
            (
                (rows_hbm, rows),
                (classes_hbm, classes),
                (cinv_hbm, cinv),
                (mode_x_hbm, mode_x),
                (mode_y_hbm, mode_y),
                (mode_z_hbm, mode_z),
                (eigen_hbm, eigen),
                (loads_hbm, loads),
            )
        )
    ]
    for fetch in fetches:
        fetch.start()
    barrier = pltpu.get_barrier_semaphore()

    def greet_sub(s):
        pl.semaphore_signal(
            barrier, inc=1, device_id=(lax.rem(me + s, n_sub), col), device_id_type=MESH
        )

    def greet_col(s):
        pl.semaphore_signal(
            barrier, inc=1, device_id=(me, lax.rem(col + s, n_col)), device_id_type=MESH
        )

    each(1, n_sub, greet_sub)
    each(1, n_col, greet_col)

    spots = (
        (lax.rem(me + 1, n_sub), col),
        (lax.rem(me + n_sub - 1, n_sub), col),
        (me, lax.rem(col + 1, n_col)),
        (me, lax.rem(col + n_col - 1, n_col)),
    )
    signs = [
        jnp.where(me * n_col + col < s * n_col + c, 1.0, -1.0).astype(F32) for s, c in spots
    ]
    match = [
        [
            jnp.where(
                jnp.logical_and(partner[0, 0, 0, k] == s, partner[0, 0, 1, k] == c), 1, 0
            ).astype(jnp.int32)
            for k in range(4)
        ]
        for s, c in spots
    ]

    fetches[0].wait()

    for d in range(4):
        picked = match[d][0] * rows[0, 0, 0:1, :]
        for k in range(1, 4):
            picked = picked + match[d][k] * rows[0, 0, k : k + 1, :]
        node_z[d] = lax.bitwise_and(picked, size_z - 1)
        node_p[d] = lax.shift_right_logical(picked, z_shift)

    def lanes(d, at):
        return pl.ds(pl.multiple_of(d * width + at, 128), CHUNK)

    def over_directions(body):
        lax.fori_loop(0, 4, lambda d, c: (body(d), c)[1], 0)

    def fill_onehot(d):
        for at in range(0, width, CHUNK):
            hit = iota((plane, CHUNK), 0) == node_p[d, :, at : at + CHUNK]
            onehot[:, lanes(d, at)] = jnp.where(hit, 1.0, 0.0).astype(BF)

    def fill_masks(d):
        for at in range(0, width, CHUNK):
            hit = iota((size_z, CHUNK), 0) == node_z[d, :, at : at + CHUNK]
            masks[:, lanes(d, at)] = jnp.where(hit, 1.0, 0.0).astype(BF)

    over_directions(fill_onehot)

    size_bz = classes.shape[4]
    blocks_y = classes.shape[3]
    blocks_x = classes.shape[2]
    for fetch in fetches[1:]:
        fetch.wait()
    el_ref[...] = jnp.zeros_like(el_ref)
    for bx in range(blocks_x):
        ids = classes[0, 0, bx]
        value = jnp.zeros(ids.shape, F32)
        for n in range(coefficients.shape[0]):
            value = jnp.where(ids == n, coefficients[n], value)
        el_ref[bx * blocks_y : (bx + 1) * blocks_y, 0:size_bz] = value
    el_t = el_ref[...].T[:size_bz, : blocks_x * blocks_y]
    plane_at = iota((blocks_x * blocks_y, plane), 1)
    block_at = lax.shift_right_logical(plane_at, y_shift + 2) * blocks_y
    block_at = block_at + lax.shift_right_logical(lax.bitwise_and(plane_at, size_y - 1), 2)
    spread = jnp.where(iota((blocks_x * blocks_y, plane), 0) == block_at, 1.0, 0.0)
    coef_block = exact_dot(el_t, spread)
    spread_z = jnp.where(
        lax.shift_right_logical(iota((size_z, size_bz), 0), 2) == iota((size_z, size_bz), 1), 1.0, 0.0
    )
    root = exact_dot(spread_z, 1.0 / jnp.sqrt(coef_block))
    root_ref[...] = root

    def copy_of(turn, d):
        down, along = d % 2, d // 2
        opposite = d + 1 - 2 * down
        to_sub = lax.rem(me + (1 - along) * (1 + down * (n_sub - 2)), n_sub)
        to_col = lax.rem(col + along * (1 + down * (n_col - 2)), n_col)
        return pltpu.make_async_remote_copy(
            src_ref=send_v.at[turn, d],
            dst_ref=recv_v.at[turn, opposite],
            send_sem=send_sem.at[turn, d],
            recv_sem=recv_sem.at[turn, opposite],
            device_id=(to_sub, to_col),
            device_id_type=MESH,
        )

    def gather(fields):
        stacked = [half for _, field, _ in fields for half in halves(field)]
        stacked = jnp.concatenate(stacked, axis=0)

        def one(d):
            for at in range(0, width, CHUNK):
                part = jnp.dot(
                    stacked,
                    onehot[:, lanes(d, at)],
                    preferred_element_type=F32,
                )
                first = 0
                for turn, field, shift in fields:
                    depth = field.shape[0]
                    both = part[first : first + depth]
                    both = both + part[first + depth : first + 2 * depth]
                    first += 2 * depth
                    at_z = lax.shift_right_logical(node_z[d, :, at : at + CHUNK], shift)
                    hit = iota((depth, CHUNK), 0) == at_z
                    send_v[turn, d, :, at : at + CHUNK] = jnp.sum(
                        jnp.where(hit, both, 0.0), axis=0, keepdims=True
                    )
            for turn, _, _ in fields:
                copy_of(turn, d).start()

        over_directions(one)

    def of_x(i):
        return lax.shift_right_logical(i, y_shift)

    def of_y(i):
        return lax.bitwise_and(i, size_y - 1)

    def expand(mode, of):
        size = mode.shape[0]
        left = jnp.where(of(iota((plane, size), 0)) == iota((plane, size), 1), 1.0, 0.0)
        right = jnp.where(of(iota((size, plane), 1)) == iota((size, plane), 0), 1.0, 0.0)
        left, right = left.astype(BF), right.astype(BF)
        parts = [
            jnp.dot(
                jnp.dot(left, part, preferred_element_type=F32).astype(BF),
                right,
                preferred_element_type=F32,
            )
            for part in halves(mode)
        ]
        return parts[0] + parts[1]

    pair = expand(mode_x[0, 0], of_x) * expand(mode_y[0, 0], of_y)
    side = mode_z[0, 0]
    pair_f[...] = right_operand(pair)
    pair_b[...] = right_operand(pair.T)
    side_f[...] = left_operand(side.T)
    side_b[...] = left_operand(side)

    spectrum = eigen[0]
    modes = spectrum.shape[1]
    mode_at = iota((modes, plane), 0)
    to_plane = jnp.logical_or(
        mode_at == of_x(iota((modes, plane), 1)),
        mode_at == size_x + of_y(iota((modes, plane), 1)),
    )
    plane_eigen = exact_dot(
        jnp.broadcast_to(spectrum, (8, modes)), jnp.where(to_plane, 1.0, 0.0)
    )[0:1]
    z_at = iota((size_z, modes), 0) + size_x + size_y == iota((size_z, modes), 1)
    z_eigen = jnp.sum(jnp.where(z_at, spectrum, 0.0), axis=1, keepdims=True)
    lam_ref[...] = 1.0 / (z_eigen + plane_eigen)

    def forward(field):
        mixed = times(field * root_ref[...], pair_f[...])
        return jnp.dot(side_f[...], right_operand(mixed), preferred_element_type=F32)

    def backward(spectral):
        mixed = times(spectral, pair_b[...])
        return root_ref[...] * jnp.dot(
            side_b[...], right_operand(mixed), preferred_element_type=F32
        )

    load_field = backward(lam_ref[...] * forward(loads[0, 0].reshape(plane, size_z).T))
    pl.semaphore_wait(barrier, n_sub - 1 + n_col - 1)

    def cinv_copy(s):
        return pltpu.make_async_remote_copy(
            src_ref=cinv,
            dst_ref=cfull.at[col],
            send_sem=cinv_send.at[s],
            recv_sem=cinv_recv.at[s],
            device_id=(me, lax.rem(col + s, n_col)),
            device_id_type=MESH,
        )

    each(1, n_col, lambda s: cinv_copy(s).start())
    cfull[col] = cinv[...]
    gather([(0, coef_block, 2), (1, load_field, 0)])
    over_directions(fill_masks)

    lane_z = iota((corners, size_z), 1)
    lane_p = iota((corners, plane), 1)
    lane_n = iota((corners, padded), 1)
    at_z = jnp.zeros((corners, size_z), jnp.int32)
    at_p = jnp.zeros((corners, plane), jnp.int32)
    at_n = jnp.zeros((corners, padded), jnp.int32)
    for t in range(corners):
        node = corner_row[0, 0, t]
        at_z = jnp.where(iota((corners, size_z), 0) == t, node, at_z)
        at_p = jnp.where(iota((corners, plane), 0) == t, node, at_p)
        at_n = jnp.where(iota((corners, padded), 0) == t, corner_id[0, 0, t], at_n)
    pick_z = jnp.where(lax.bitwise_and(at_z, size_z - 1) == lane_z, 1.0, 0.0)
    pick_p = jnp.where(lax.shift_right_logical(at_p, z_shift) == lane_p, 1.0, 0.0)
    pick_n = jnp.where(at_n == lane_n, 1.0, 0.0)
    corner_root = jnp.sum(exact_dot(pick_z, root) * pick_p, axis=1, keepdims=True)
    corner_z = exact_dot(pick_z, side)
    corner_p = exact_dot(pick_p, pair) * corner_root
    high, low = halves(corner_z)
    pad_ref[...] = jnp.zeros_like(pad_ref)
    pad_ref[0:corners, :] = high.astype(F32)
    pad_ref[corners : 2 * corners, :] = high.astype(F32)
    pad_ref[2 * corners : 3 * corners, :] = low.astype(F32)
    corner_l[...] = pad_ref[...].T.astype(BF)
    corner_z3 = jnp.concatenate([high.astype(F32), high.astype(F32), low.astype(F32)], axis=1)
    corner_z3 = corner_z3.astype(BF)

    def all_sum(turn, vector):
        vec_sub[turn, 0] = vector

        def sub_copy(s):
            return pltpu.make_async_remote_copy(
                src_ref=vec_sub.at[turn, 0],
                dst_ref=vec_sub.at[turn, s],
                send_sem=sub_send.at[turn, s],
                recv_sem=sub_recv.at[turn, s],
                device_id=(lax.rem(me + s, n_sub), col),
                device_id_type=MESH,
            )

        def col_copy(s):
            return pltpu.make_async_remote_copy(
                src_ref=mine_col.at[turn],
                dst_ref=vec_col.at[turn, s],
                send_sem=col_send.at[turn, s],
                recv_sem=col_recv.at[turn, s],
                device_id=(me, lax.rem(col + s, n_col)),
                device_id_type=MESH,
            )

        each(1, n_sub, lambda s: sub_copy(s).start())
        each(1, n_sub, lambda s: sub_copy(s).wait())
        mine = jnp.sum(vec_sub[turn], axis=0)
        mine_col[turn] = mine
        each(1, n_col, lambda s: col_copy(s).start())
        vec_col[turn, 0] = mine
        each(1, n_col, lambda s: col_copy(s).wait())
        return jnp.sum(vec_col[turn], axis=0)

    def receive(turn):
        for d in range(4):
            copy_of(turn, d).wait()

    def jump(turn):
        receive(turn)
        return [signs[d] * (send_v[turn, d] - recv_v[turn, d]) for d in range(4)]

    def scatter(values):
        for d in range(4):
            scaled[d] = signs[d] * values[d]

        def one(d, total):
            high, low = halves(scaled[d])
            for at in range(0, width, CHUNK):
                mask = masks[:, lanes(d, at)]
                placed_rows[:size_z, at : at + CHUNK] = mask * high[:, at : at + CHUNK]
                placed_rows[size_z:, at : at + CHUNK] = mask * low[:, at : at + CHUNK]
            return total + lax.dot_general(
                placed_rows[...],
                onehot[:, pl.ds(pl.multiple_of(d * width, 128), width)],
                (((1,), (1,)), ((), ())),
                preferred_element_type=F32,
            )

        total = lax.fori_loop(0, 4, one, jnp.zeros((2 * size_z, plane), F32))
        return total[:size_z] + total[size_z:]

    def all_of(x):
        return jnp.sum(jnp.sum(x, axis=0, keepdims=True), axis=1, keepdims=True)

    def dot4(a, b):
        total = a[0] * b[0]
        for d in range(1, 4):
            total = total + a[d] * b[d]
        return jnp.sum(total, axis=1, keepdims=True)

    first_row = iota((corners, padded), 0) == 0

    def apply(turn, values, scalars):
        modal = forward(scatter(values))
        spectral = lam_ref[...] * modal
        energy = all_of(modal * spectral)
        at_corner = jnp.sum(
            jnp.dot(corner_z3, right_operand(spectral), preferred_element_type=F32) * corner_p,
            axis=1,
            keepdims=True,
        )
        vector = pick_n * at_corner
        for n, scalar in enumerate([energy] + scalars):
            here = jnp.logical_and(first_row, lane_n == total_corners + n)
            vector = jnp.where(here, scalar, vector)
        summed = all_sum(turn - 2, vector)
        if turn == 2:
            each(1, n_col, lambda s: cinv_copy(s).wait())
        inverse = cfull[...].reshape(total_corners, total_corners)
        coarse = jnp.sum(exact_dot(summed[:, :total_corners], inverse), axis=0, keepdims=True)
        total = jnp.sum(summed, axis=0, keepdims=True)
        quad = jnp.sum(total[:, :total_corners] * coarse, axis=1, keepdims=True)
        local = jnp.sum(pick_n[:, :total_corners] * coarse, axis=1, keepdims=True)
        high, low = halves(corner_p * local)
        high, low = high.astype(F32), low.astype(F32)
        rest = jnp.zeros((size_z - 3 * corners, plane), F32)
        source = jnp.concatenate([high, low, high, rest], axis=0).astype(BF)
        extra = jnp.dot(corner_l[...], source, preferred_element_type=F32)
        gather([(turn, backward(spectral + lam_ref[...] * extra), 0)])
        lane = iota((1, padded), 1)
        got = [
            jnp.sum(jnp.where(lane == total_corners + n, total, 0.0), axis=1, keepdims=True)
            for n in range(1 + len(scalars))
        ]
        return 2.0 * (got[0] + quad), got[1:]

    receive(0)
    weight = []
    for d in range(4):
        near, far = send_v[0, d], recv_v[0, d]
        weight.append(near * far / (near + far))
    four = range(4)
    resid = jump(1)
    direction = [weight[d] * resid[d] for d in four]
    image_dot, (rz,) = apply(2, direction, [dot4(resid, direction)])
    alpha = rz / image_dot
    mult = [alpha * direction[d] for d in four]
    image = jump(2)
    for step in range(1, ITERS):
        resid = [resid[d] - alpha * image[d] for d in four]
        precond = [weight[d] * resid[d] for d in four]
        own_dot, (rz_next, cross) = apply(
            2 + step, precond, [dot4(resid, precond), dot4(precond, image)]
        )
        beta = rz_next / rz
        image_dot = own_dot + 2.0 * beta * cross + beta * beta * image_dot
        alpha = rz_next / image_dot
        rz = rz_next
        direction = [precond[d] + beta * direction[d] for d in four]
        mult = [mult[d] + alpha * direction[d] for d in four]
        fresh = jump(2 + step)
        image = [fresh[d] + beta * image[d] for d in four]
    resid = [resid[d] - alpha * image[d] for d in four]
    for k in range(4):
        share = [match[d][k].astype(F32) for d in four]
        one = share[0] * mult[0]
        two = share[0] * resid[0]
        for d in range(1, 4):
            one = one + share[d] * mult[d]
            two = two + share[d] * resid[d]
        out_mult[0, 0, k : k + 1, :] = one
        out_resid[0, 0, k : k + 1, :] = two


def on_device(n_sub, n_col, *args):
    args = list(args)
    args[7] = jnp.swapaxes(args[7], 2, 3)
    loads, mode_x, mode_y, mode_z, eigen, classes = args[:6]
    rows, cinv = args[8], args[11]
    size_z = mode_z.shape[2]
    plane = mode_x.shape[2] * mode_y.shape[2]
    width = rows.shape[3]
    corners = args[10].shape[2]
    total_corners = cinv.shape[1]
    padded = -(-(total_corners + 3) // 128) * 128
    turns = 2 + ITERS
    vmem = pl.BlockSpec(memory_space=pltpu.VMEM)
    hbm = pl.BlockSpec(memory_space=pltpu.HBM)
    smem = pl.BlockSpec(memory_space=pltpu.SMEM)
    dma = pltpu.SemaphoreType.DMA
    out = jax.ShapeDtypeStruct(rows.shape, F32)
    return pl.pallas_call(
        functools.partial(kernel, n_sub, n_col),
        out_shape=(out, out),
        in_specs=[hbm] * 6 + [smem] * 2 + [hbm] + [smem] * 2 + [hbm],
        out_specs=(vmem, vmem),
        scratch_shapes=[
            *[
                pltpu.VMEM(x.shape, x.dtype)
                for x in (loads, mode_x, mode_y, mode_z, eigen, classes, rows, cinv)
            ],
            dma((8,)),
            pltpu.VMEM((plane, 4 * width), BF),
            pltpu.VMEM((size_z, 4 * width), BF),
            pltpu.VMEM((2 * size_z, width), BF),
            pltpu.VMEM((4, 1, width), jnp.int32),
            pltpu.VMEM((4, 1, width), jnp.int32),
            pltpu.VMEM((4, 1, width), F32),
            pltpu.VMEM((128, 128), F32),
            pltpu.VMEM((3 * plane, plane), BF),
            pltpu.VMEM((3 * plane, plane), BF),
            pltpu.VMEM((size_z, 3 * size_z), BF),
            pltpu.VMEM((size_z, 3 * size_z), BF),
            pltpu.VMEM((size_z, plane), F32),
            pltpu.VMEM((size_z, plane), F32),
            pltpu.VMEM((size_z, size_z), BF),
            pltpu.VMEM((size_z, size_z), F32),
            pltpu.VMEM((n_col,) + cinv.shape, F32),
            pltpu.VMEM((turns, 4, 1, width), F32),
            pltpu.VMEM((turns, 4, 1, width), F32),
            pltpu.VMEM((ITERS, n_sub, corners, padded), F32),
            pltpu.VMEM((ITERS, n_col, corners, padded), F32),
            pltpu.VMEM((ITERS, corners, padded), F32),
            dma((turns, 4)),
            dma((turns, 4)),
            dma((ITERS, n_sub)),
            dma((ITERS, n_sub)),
            dma((ITERS, n_col)),
            dma((ITERS, n_col)),
            dma((n_col,)),
            dma((n_col,)),
        ],
        compiler_params=pltpu.CompilerParams(
            collective_id=0, has_side_effects=True, vmem_limit_bytes=60 * 1024 * 1024
        ),
        name="feti_pcg",
    )(*args)


def solution(mesh):
    placed = (
        P("sub", "coarse", None, None, None),
        P("sub", "coarse", None, None),
        P("sub", "coarse", None, None),
        P("sub", "coarse", None, None),
        P("sub", "coarse", None),
        P("sub", "coarse", None, None, None),
        P(),
        P("sub", "coarse", None, None),
        P("sub", "coarse", None, None),
        P("sub", "coarse", None),
        P("sub", "coarse", None),
        P("coarse", None),
    )
    return jax.shard_map(
        functools.partial(on_device, mesh.shape["sub"], mesh.shape["coarse"]),
        mesh=mesh,
        in_specs=placed,
        out_specs=(P("sub", "coarse", None, None), P("sub", "coarse", None, None)),
        check_vma=False,
    )
```

```python
import functools

import jax
import jax.numpy as jnp
from jax import lax
from jax.experimental import pallas as pl
from jax.experimental.pallas import tpu as pltpu
from jax.sharding import PartitionSpec as P

ITERS = 2
CHUNK = 512
DIRECT = 64
BF = jnp.bfloat16
F32 = jnp.float32
HI = lax.Precision.HIGHEST
MESH = pl.DeviceIdType.MESH


def exact_dot(a, b):
    return jnp.dot(a, b, precision=HI, preferred_element_type=F32)


def halves(x):
    high = x.astype(BF)
    return high, (x - high.astype(F32)).astype(BF)


def iota(shape, dim):
    return lax.broadcasted_iota(jnp.int32, shape, dim)


def each(low, high, body):
    if high - low <= 8:
        for i in range(low, high):
            body(i)
    else:
        lax.fori_loop(low, high, lambda i, c: (body(i), c)[1], 0)


def right_operand(x):
    high, low = halves(x)
    return jnp.concatenate([high, low, high], axis=0)


def left_operand(x):
    high, low = halves(x)
    return jnp.concatenate([high, high, low], axis=1)


def times(x, right):
    return jnp.dot(left_operand(x), right, preferred_element_type=F32)


def kernel(
    n_sub,
    n_col,
    loads_hbm,
    mode_x_hbm,
    mode_y_hbm,
    mode_z_hbm,
    eigen_hbm,
    classes_hbm,
    coefficients,
    partner,
    rows_hbm,
    corner_id,
    corner_row,
    cinv_hbm,
    out_mult,
    out_resid,
    loads,
    mode_x,
    mode_y,
    mode_z,
    eigen,
    classes,
    rows,
    cinv,
    load_sem,
    onehot,
    masks,
    placed_rows,
    node_z,
    node_p,
    scaled,
    el_ref,
    pair_f,
    pair_b,
    side_f,
    side_b,
    lam_ref,
    root_ref,
    corner_l,
    pad_ref,
    cfull,
    own_rows,
    send_v,
    recv_v,
    vec_sub,
    vec_col,
    mine_col,
    send_sem,
    recv_sem,
    sub_send,
    sub_recv,
    col_send,
    col_recv,
    cinv_send,
    cinv_recv,
):
    me = lax.axis_index("sub")
    col = lax.axis_index("coarse")
    size_x = mode_x.shape[2]
    size_y = mode_y.shape[2]
    size_z = mode_z.shape[2]
    plane = size_x * size_y
    width = rows.shape[3]
    corners = corner_row.shape[2]
    total_corners = cinv.shape[1]
    padded = vec_sub.shape[3]
    z_shift = size_z.bit_length() - 1
    y_shift = size_y.bit_length() - 1
    assert size_z == 1 << z_shift and size_y == 1 << y_shift

    fetches = [
        pltpu.make_async_copy(source, target, load_sem.at[n])
        for n, (source, target) in enumerate(
            (
                (rows_hbm, rows),
                (classes_hbm, classes),
                (cinv_hbm, cinv),
                (mode_x_hbm, mode_x),
                (mode_y_hbm, mode_y),
                (mode_z_hbm, mode_z),
                (eigen_hbm, eigen),
                (loads_hbm, loads),
            )
        )
    ]
    for fetch in fetches:
        fetch.start()
    barrier = pltpu.get_barrier_semaphore()

    def greet_sub(s):
        pl.semaphore_signal(
            barrier, inc=1, device_id=(lax.rem(me + s, n_sub), col), device_id_type=MESH
        )

    def greet_col(s):
        pl.semaphore_signal(
            barrier, inc=1, device_id=(me, lax.rem(col + s, n_col)), device_id_type=MESH
        )

    n_all = n_sub * n_col
    direct = n_all <= DIRECT
    own = me * n_col + col

    def other(s):
        flat = lax.rem(own + s, n_all)
        return flat // n_col, lax.rem(flat, n_col)

    def greet_all(s):
        pl.semaphore_signal(barrier, inc=1, device_id=other(s), device_id_type=MESH)

    if direct:
        each(1, n_all, greet_all)
    else:
        each(1, n_sub, greet_sub)
        each(1, n_col, greet_col)

    spots = (
        (lax.rem(me + 1, n_sub), col),
        (lax.rem(me + n_sub - 1, n_sub), col),
        (me, lax.rem(col + 1, n_col)),
        (me, lax.rem(col + n_col - 1, n_col)),
    )
    signs = [
        jnp.where(me * n_col + col < s * n_col + c, 1.0, -1.0).astype(F32) for s, c in spots
    ]
    match = [
        [
            jnp.where(
                jnp.logical_and(partner[0, 0, 0, k] == s, partner[0, 0, 1, k] == c), 1, 0
            ).astype(jnp.int32)
            for k in range(4)
        ]
        for s, c in spots
    ]

    fetches[0].wait()

    for d in range(4):
        picked = match[d][0] * rows[0, 0, 0:1, :]
        for k in range(1, 4):
            picked = picked + match[d][k] * rows[0, 0, k : k + 1, :]
        node_z[d] = lax.bitwise_and(picked, size_z - 1)
        node_p[d] = lax.shift_right_logical(picked, z_shift)

    def lanes(d, at):
        return pl.ds(pl.multiple_of(d * width + at, 128), CHUNK)

    def over_directions(body):
        lax.fori_loop(0, 4, lambda d, c: (body(d), c)[1], 0)

    def fill_onehot(d):
        for at in range(0, width, CHUNK):
            hit = iota((plane, CHUNK), 0) == node_p[d, :, at : at + CHUNK]
            onehot[:, lanes(d, at)] = jnp.where(hit, 1.0, 0.0).astype(BF)

    def fill_masks(d):
        for at in range(0, width, CHUNK):
            hit = iota((size_z, CHUNK), 0) == node_z[d, :, at : at + CHUNK]
            masks[:, lanes(d, at)] = jnp.where(hit, 1.0, 0.0).astype(BF)

    over_directions(fill_onehot)

    size_bz = classes.shape[4]
    blocks_y = classes.shape[3]
    blocks_x = classes.shape[2]
    for fetch in fetches[1:]:
        fetch.wait()
    el_ref[...] = jnp.zeros_like(el_ref)
    for bx in range(blocks_x):
        ids = classes[0, 0, bx]
        value = jnp.zeros(ids.shape, F32)
        for n in range(coefficients.shape[0]):
            value = jnp.where(ids == n, coefficients[n], value)
        el_ref[bx * blocks_y : (bx + 1) * blocks_y, 0:size_bz] = value
    el_t = el_ref[...].T[:size_bz, : blocks_x * blocks_y]
    plane_at = iota((blocks_x * blocks_y, plane), 1)
    block_at = lax.shift_right_logical(plane_at, y_shift + 2) * blocks_y
    block_at = block_at + lax.shift_right_logical(lax.bitwise_and(plane_at, size_y - 1), 2)
    spread = jnp.where(iota((blocks_x * blocks_y, plane), 0) == block_at, 1.0, 0.0)
    coef_block = exact_dot(el_t, spread)
    spread_z = jnp.where(
        lax.shift_right_logical(iota((size_z, size_bz), 0), 2) == iota((size_z, size_bz), 1), 1.0, 0.0
    )
    root = exact_dot(spread_z, 1.0 / jnp.sqrt(coef_block))
    root_ref[...] = root

    def copy_of(turn, d):
        down, along = d % 2, d // 2
        opposite = d + 1 - 2 * down
        to_sub = lax.rem(me + (1 - along) * (1 + down * (n_sub - 2)), n_sub)
        to_col = lax.rem(col + along * (1 + down * (n_col - 2)), n_col)
        return pltpu.make_async_remote_copy(
            src_ref=send_v.at[turn, d],
            dst_ref=recv_v.at[turn, opposite],
            send_sem=send_sem.at[turn, d],
            recv_sem=recv_sem.at[turn, opposite],
            device_id=(to_sub, to_col),
            device_id_type=MESH,
        )

    def gather(fields):
        stacked = [half for _, field, _ in fields for half in halves(field)]
        stacked = jnp.concatenate(stacked, axis=0)

        def one(d):
            for at in range(0, width, CHUNK):
                part = jnp.dot(
                    stacked,
                    onehot[:, lanes(d, at)],
                    preferred_element_type=F32,
                )
                first = 0
                for turn, field, shift in fields:
                    depth = field.shape[0]
                    both = part[first : first + depth]
                    both = both + part[first + depth : first + 2 * depth]
                    first += 2 * depth
                    at_z = lax.shift_right_logical(node_z[d, :, at : at + CHUNK], shift)
                    hit = iota((depth, CHUNK), 0) == at_z
                    send_v[turn, d, :, at : at + CHUNK] = jnp.sum(
                        jnp.where(hit, both, 0.0), axis=0, keepdims=True
                    )
            for turn, _, _ in fields:
                copy_of(turn, d).start()

        over_directions(one)

    def of_x(i):
        return lax.shift_right_logical(i, y_shift)

    def of_y(i):
        return lax.bitwise_and(i, size_y - 1)

    def expand(mode, of):
        size = mode.shape[0]
        left = jnp.where(of(iota((plane, size), 0)) == iota((plane, size), 1), 1.0, 0.0)
        right = jnp.where(of(iota((size, plane), 1)) == iota((size, plane), 0), 1.0, 0.0)
        left, right = left.astype(BF), right.astype(BF)
        parts = [
            jnp.dot(
                jnp.dot(left, part, preferred_element_type=F32).astype(BF),
                right,
                preferred_element_type=F32,
            )
            for part in halves(mode)
        ]
        return parts[0] + parts[1]

    pair = expand(mode_x[0, 0], of_x) * expand(mode_y[0, 0], of_y)
    side = mode_z[0, 0]
    pair_f[...] = right_operand(pair)
    pair_b[...] = right_operand(pair.T)
    side_f[...] = left_operand(side.T)
    side_b[...] = left_operand(side)

    spectrum = eigen[0]
    modes = spectrum.shape[1]
    mode_at = iota((modes, plane), 0)
    to_plane = jnp.logical_or(
        mode_at == of_x(iota((modes, plane), 1)),
        mode_at == size_x + of_y(iota((modes, plane), 1)),
    )
    plane_eigen = exact_dot(
        jnp.broadcast_to(spectrum, (8, modes)), jnp.where(to_plane, 1.0, 0.0)
    )[0:1]
    z_at = iota((size_z, modes), 0) + size_x + size_y == iota((size_z, modes), 1)
    z_eigen = jnp.sum(jnp.where(z_at, spectrum, 0.0), axis=1, keepdims=True)
    lam_ref[...] = 1.0 / (z_eigen + plane_eigen)

    def forward(field):
        mixed = times(field * root_ref[...], pair_f[...])
        return jnp.dot(side_f[...], right_operand(mixed), preferred_element_type=F32)

    def backward(spectral):
        mixed = times(spectral, pair_b[...])
        return root_ref[...] * jnp.dot(
            side_b[...], right_operand(mixed), preferred_element_type=F32
        )

    load_field = backward(lam_ref[...] * forward(loads[0, 0].reshape(plane, size_z).T))
    pl.semaphore_wait(barrier, n_all - 1 if direct else n_sub - 1 + n_col - 1)

    def cinv_copy(s):
        return pltpu.make_async_remote_copy(
            src_ref=cinv,
            dst_ref=cfull.at[col],
            send_sem=cinv_send.at[s],
            recv_sem=cinv_recv.at[s],
            device_id=(me, lax.rem(col + s, n_col)),
            device_id_type=MESH,
        )

    each(1, n_col, lambda s: cinv_copy(s).start())
    cfull[col] = cinv[...]
    gather([(0, coef_block, 2), (1, load_field, 0)])
    over_directions(fill_masks)

    lane_z = iota((corners, size_z), 1)
    lane_p = iota((corners, plane), 1)
    lane_n = iota((corners, padded), 1)
    at_z = jnp.zeros((corners, size_z), jnp.int32)
    at_p = jnp.zeros((corners, plane), jnp.int32)
    at_n = jnp.zeros((corners, padded), jnp.int32)
    for t in range(corners):
        node = corner_row[0, 0, t]
        at_z = jnp.where(iota((corners, size_z), 0) == t, node, at_z)
        at_p = jnp.where(iota((corners, plane), 0) == t, node, at_p)
        at_n = jnp.where(iota((corners, padded), 0) == t, corner_id[0, 0, t], at_n)
    pick_z = jnp.where(lax.bitwise_and(at_z, size_z - 1) == lane_z, 1.0, 0.0)
    pick_p = jnp.where(lax.shift_right_logical(at_p, z_shift) == lane_p, 1.0, 0.0)
    pick_n = jnp.where(at_n == lane_n, 1.0, 0.0)
    corner_root = jnp.sum(exact_dot(pick_z, root) * pick_p, axis=1, keepdims=True)
    corner_z = exact_dot(pick_z, side)
    corner_p = exact_dot(pick_p, pair) * corner_root
    high, low = halves(corner_z)
    pad_ref[...] = jnp.zeros_like(pad_ref)
    pad_ref[0:corners, :] = high.astype(F32)
    pad_ref[corners : 2 * corners, :] = high.astype(F32)
    pad_ref[2 * corners : 3 * corners, :] = low.astype(F32)
    corner_l[...] = pad_ref[...].T.astype(BF)
    corner_z3 = jnp.concatenate([high.astype(F32), high.astype(F32), low.astype(F32)], axis=1)
    corner_z3 = corner_z3.astype(BF)

    def sum_copies(turn):
        count = n_all if direct else n_sub

        def copy(s):
            return pltpu.make_async_remote_copy(
                src_ref=vec_sub.at[turn, 0],
                dst_ref=vec_sub.at[turn, s],
                send_sem=sub_send.at[turn, s],
                recv_sem=sub_recv.at[turn, s],
                device_id=other(s) if direct else (lax.rem(me + s, n_sub), col),
                device_id_type=MESH,
            )

        return count, copy

    def sum_start(turn, vector):
        vec_sub[turn, 0] = vector
        count, copy = sum_copies(turn)
        each(1, count, lambda s: copy(s).start())

    def sum_finish(turn):
        count, copy = sum_copies(turn)
        each(1, count, lambda s: copy(s).wait())
        mine = jnp.sum(vec_sub[turn], axis=0)
        if direct:
            return mine
        mine_col[turn] = mine

        def col_copy(s):
            return pltpu.make_async_remote_copy(
                src_ref=mine_col.at[turn],
                dst_ref=vec_col.at[turn, s],
                send_sem=col_send.at[turn, s],
                recv_sem=col_recv.at[turn, s],
                device_id=(me, lax.rem(col + s, n_col)),
                device_id_type=MESH,
            )

        each(1, n_col, lambda s: col_copy(s).start())
        vec_col[turn, 0] = mine
        each(1, n_col, lambda s: col_copy(s).wait())
        return jnp.sum(vec_col[turn], axis=0)

    def receive(turn):
        for d in range(4):
            copy_of(turn, d).wait()

    def jump(turn):
        receive(turn)
        return [signs[d] * (send_v[turn, d] - recv_v[turn, d]) for d in range(4)]

    def scatter(values):
        for d in range(4):
            scaled[d] = signs[d] * values[d]

        def one(d, total):
            high, low = halves(scaled[d])
            for at in range(0, width, CHUNK):
                mask = masks[:, lanes(d, at)]
                placed_rows[:size_z, at : at + CHUNK] = mask * high[:, at : at + CHUNK]
                placed_rows[size_z:, at : at + CHUNK] = mask * low[:, at : at + CHUNK]
            return total + lax.dot_general(
                placed_rows[...],
                onehot[:, pl.ds(pl.multiple_of(d * width, 128), width)],
                (((1,), (1,)), ((), ())),
                preferred_element_type=F32,
            )

        total = lax.fori_loop(0, 4, one, jnp.zeros((2 * size_z, plane), F32))
        return total[:size_z] + total[size_z:]

    def all_of(x):
        return jnp.sum(jnp.sum(x, axis=0, keepdims=True), axis=1, keepdims=True)

    def dot4(a, b):
        total = a[0] * b[0]
        for d in range(1, 4):
            total = total + a[d] * b[d]
        return jnp.sum(total, axis=1, keepdims=True)

    lane = iota((1, padded), 1)

    def apply(turn, values, scalars):
        modal = forward(scatter(values))
        spectral = lam_ref[...] * modal
        energy = all_of(modal * spectral)
        at_corner = jnp.sum(
            jnp.dot(corner_z3, right_operand(spectral), preferred_element_type=F32) * corner_p,
            axis=1,
            keepdims=True,
        )
        vector = jnp.sum(pick_n * at_corner, axis=0, keepdims=True)
        for n, scalar in enumerate([energy] + scalars):
            vector = jnp.where(lane == total_corners + n, scalar, vector)
        sum_start(turn - 2, vector)
        if turn == 2:
            each(1, n_col, lambda s: cinv_copy(s).wait())
            inverse = cfull[...].reshape(total_corners, total_corners)
            own_rows[...] = exact_dot(pick_n[:, :total_corners], inverse)
        total = sum_finish(turn - 2)
        at_corners = total[:, :total_corners]
        local = jnp.sum(own_rows[...] * at_corners, axis=1, keepdims=True)
        high, low = halves(corner_p * local)
        high, low = high.astype(F32), low.astype(F32)
        rest = jnp.zeros((size_z - 3 * corners, plane), F32)
        source = jnp.concatenate([high, low, high, rest], axis=0).astype(BF)
        extra = jnp.dot(corner_l[...], source, preferred_element_type=F32)
        gather([(turn, backward(spectral + lam_ref[...] * extra), 0)])
        inverse = cfull[...].reshape(total_corners, total_corners)
        coarse = exact_dot(jnp.broadcast_to(at_corners, (8, total_corners)), inverse)[0:1]
        quad = jnp.sum(at_corners * coarse, axis=1, keepdims=True)
        got = [
            jnp.sum(jnp.where(lane == total_corners + n, total, 0.0), axis=1, keepdims=True)
            for n in range(1 + len(scalars))
        ]
        return 2.0 * (got[0] + quad), got[1:]

    receive(0)
    weight = []
    for d in range(4):
        near, far = send_v[0, d], recv_v[0, d]
        weight.append(near * far / (near + far))
    four = range(4)
    resid = jump(1)
    direction = [weight[d] * resid[d] for d in four]
    image_dot, (rz,) = apply(2, direction, [dot4(resid, direction)])
    alpha = rz / image_dot
    mult = [alpha * direction[d] for d in four]
    image = jump(2)
    for step in range(1, ITERS):
        resid = [resid[d] - alpha * image[d] for d in four]
        precond = [weight[d] * resid[d] for d in four]
        own_dot, (rz_next, cross) = apply(
            2 + step, precond, [dot4(resid, precond), dot4(precond, image)]
        )
        beta = rz_next / rz
        image_dot = own_dot + 2.0 * beta * cross + beta * beta * image_dot
        alpha = rz_next / image_dot
        rz = rz_next
        direction = [precond[d] + beta * direction[d] for d in four]
        mult = [mult[d] + alpha * direction[d] for d in four]
        fresh = jump(2 + step)
        image = [fresh[d] + beta * image[d] for d in four]
    resid = [resid[d] - alpha * image[d] for d in four]
    for k in range(4):
        share = [match[d][k].astype(F32) for d in four]
        one = share[0] * mult[0]
        two = share[0] * resid[0]
        for d in range(1, 4):
            one = one + share[d] * mult[d]
            two = two + share[d] * resid[d]
        out_mult[0, 0, k : k + 1, :] = one
        out_resid[0, 0, k : k + 1, :] = two


def on_device(n_sub, n_col, *args):
    args = list(args)
    args[7] = jnp.swapaxes(args[7], 2, 3)
    loads, mode_x, mode_y, mode_z, eigen, classes = args[:6]
    rows, cinv = args[8], args[11]
    size_z = mode_z.shape[2]
    plane = mode_x.shape[2] * mode_y.shape[2]
    width = rows.shape[3]
    corners = args[10].shape[2]
    total_corners = cinv.shape[1]
    padded = -(-(total_corners + 3) // 128) * 128
    turns = 2 + ITERS
    first = n_sub * n_col if n_sub * n_col <= DIRECT else n_sub
    vmem = pl.BlockSpec(memory_space=pltpu.VMEM)
    hbm = pl.BlockSpec(memory_space=pltpu.HBM)
    smem = pl.BlockSpec(memory_space=pltpu.SMEM)
    dma = pltpu.SemaphoreType.DMA
    out = jax.ShapeDtypeStruct(rows.shape, F32)
    return pl.pallas_call(
        functools.partial(kernel, n_sub, n_col),
        out_shape=(out, out),
        in_specs=[hbm] * 6 + [smem] * 2 + [hbm] + [smem] * 2 + [hbm],
        out_specs=(vmem, vmem),
        scratch_shapes=[
            *[
                pltpu.VMEM(x.shape, x.dtype)
                for x in (loads, mode_x, mode_y, mode_z, eigen, classes, rows, cinv)
            ],
            dma((8,)),
            pltpu.VMEM((plane, 4 * width), BF),
            pltpu.VMEM((size_z, 4 * width), BF),
            pltpu.VMEM((2 * size_z, width), BF),
            pltpu.VMEM((4, 1, width), jnp.int32),
            pltpu.VMEM((4, 1, width), jnp.int32),
            pltpu.VMEM((4, 1, width), F32),
            pltpu.VMEM((128, 128), F32),
            pltpu.VMEM((3 * plane, plane), BF),
            pltpu.VMEM((3 * plane, plane), BF),
            pltpu.VMEM((size_z, 3 * size_z), BF),
            pltpu.VMEM((size_z, 3 * size_z), BF),
            pltpu.VMEM((size_z, plane), F32),
            pltpu.VMEM((size_z, plane), F32),
            pltpu.VMEM((size_z, size_z), BF),
            pltpu.VMEM((size_z, size_z), F32),
            pltpu.VMEM((n_col,) + cinv.shape, F32),
            pltpu.VMEM((corners, total_corners), F32),
            pltpu.VMEM((turns, 4, 1, width), F32),
            pltpu.VMEM((turns, 4, 1, width), F32),
            pltpu.VMEM((ITERS, first, 1, padded), F32),
            pltpu.VMEM((ITERS, n_col, 1, padded), F32),
            pltpu.VMEM((ITERS, 1, padded), F32),
            dma((turns, 4)),
            dma((turns, 4)),
            dma((ITERS, first)),
            dma((ITERS, first)),
            dma((ITERS, n_col)),
            dma((ITERS, n_col)),
            dma((n_col,)),
            dma((n_col,)),
        ],
        compiler_params=pltpu.CompilerParams(
            collective_id=0, has_side_effects=True, vmem_limit_bytes=60 * 1024 * 1024
        ),
        name="feti_pcg",
    )(*args)


def solution(mesh):
    placed = (
        P("sub", "coarse", None, None, None),
        P("sub", "coarse", None, None),
        P("sub", "coarse", None, None),
        P("sub", "coarse", None, None),
        P("sub", "coarse", None),
        P("sub", "coarse", None, None, None),
        P(),
        P("sub", "coarse", None, None),
        P("sub", "coarse", None, None),
        P("sub", "coarse", None),
        P("sub", "coarse", None),
        P("coarse", None),
    )
    return jax.shard_map(
        functools.partial(on_device, mesh.shape["sub"], mesh.shape["coarse"]),
        mesh=mesh,
        in_specs=placed,
        out_specs=(P("sub", "coarse", None, None), P("sub", "coarse", None, None)),
        check_vma=False,
    )
```

```python
import functools

import jax
import jax.numpy as jnp
from jax import lax
from jax.experimental import pallas as pl
from jax.experimental.pallas import tpu as pltpu
from jax.sharding import PartitionSpec as P

ITERS = 2
CHUNK = 512
DIRECT = 64
BF = jnp.bfloat16
F32 = jnp.float32
HI = lax.Precision.HIGHEST
MESH = pl.DeviceIdType.MESH


def exact_dot(a, b):
    return jnp.dot(a, b, precision=HI, preferred_element_type=F32)


def halves(x):
    high = x.astype(BF)
    return high, (x - high.astype(F32)).astype(BF)


def iota(shape, dim):
    return lax.broadcasted_iota(jnp.int32, shape, dim)


def each(low, high, body):
    if high - low <= 8:
        for i in range(low, high):
            body(i)
    else:
        lax.fori_loop(low, high, lambda i, c: (body(i), c)[1], 0)


def right_operand(x):
    high, low = halves(x)
    return jnp.concatenate([high, low, high], axis=0)


def left_operand(x):
    high, low = halves(x)
    return jnp.concatenate([high, high, low], axis=1)


def times(x, right):
    return jnp.dot(left_operand(x), right, preferred_element_type=F32)


def kernel(
    n_sub,
    n_col,
    loads_hbm,
    mode_x_hbm,
    mode_y_hbm,
    mode_z_hbm,
    eigen_hbm,
    classes_hbm,
    coefficients,
    partner,
    rows_hbm,
    corner_id,
    corner_row,
    cinv_hbm,
    out_mult,
    out_resid,
    loads,
    mode_x,
    mode_y,
    mode_z,
    eigen,
    classes,
    rows,
    cinv,
    load_sem,
    onehot,
    masks,
    placed_rows,
    node_z,
    node_p,
    el_ref,
    pair_f,
    pair_b,
    side_f,
    side_b,
    lam_ref,
    root_ref,
    corner_l,
    pad_ref,
    cfull,
    own_rows,
    send_v,
    recv_v,
    vec_sub,
    vec_col,
    mine_col,
    send_sem,
    recv_sem,
    sub_send,
    sub_recv,
    col_send,
    col_recv,
    cinv_send,
    cinv_recv,
):
    me = lax.axis_index("sub")
    col = lax.axis_index("coarse")
    size_x = mode_x.shape[2]
    size_y = mode_y.shape[2]
    size_z = mode_z.shape[2]
    plane = size_x * size_y
    width = rows.shape[3]
    corners = corner_row.shape[2]
    total_corners = cinv.shape[1]
    padded = vec_sub.shape[3]
    z_shift = size_z.bit_length() - 1
    y_shift = size_y.bit_length() - 1
    assert size_z == 1 << z_shift and size_y == 1 << y_shift

    fetches = [
        pltpu.make_async_copy(source, target, load_sem.at[n])
        for n, (source, target) in enumerate(
            (
                (rows_hbm, rows),
                (classes_hbm, classes),
                (cinv_hbm, cinv),
                (mode_x_hbm, mode_x),
                (mode_y_hbm, mode_y),
                (mode_z_hbm, mode_z),
                (eigen_hbm, eigen),
                (loads_hbm, loads),
            )
        )
    ]
    for fetch in fetches:
        fetch.start()
    barrier = pltpu.get_barrier_semaphore()

    def greet_sub(s):
        pl.semaphore_signal(
            barrier, inc=1, device_id=(lax.rem(me + s, n_sub), col), device_id_type=MESH
        )

    def greet_col(s):
        pl.semaphore_signal(
            barrier, inc=1, device_id=(me, lax.rem(col + s, n_col)), device_id_type=MESH
        )

    n_all = n_sub * n_col
    direct = n_all <= DIRECT
    own = me * n_col + col

    def other(s):
        flat = lax.rem(own + s, n_all)
        return lax.div(flat, n_col), lax.rem(flat, n_col)

    def greet_all(s):
        pl.semaphore_signal(barrier, inc=1, device_id=other(s), device_id_type=MESH)

    if direct:
        each(1, n_all, greet_all)
    else:
        each(1, n_sub, greet_sub)
        each(1, n_col, greet_col)

    spots = (
        (lax.rem(me + 1, n_sub), col),
        (lax.rem(me + n_sub - 1, n_sub), col),
        (me, lax.rem(col + 1, n_col)),
        (me, lax.rem(col + n_col - 1, n_col)),
    )
    signs = [
        jnp.where(me * n_col + col < s * n_col + c, 1.0, -1.0).astype(F32) for s, c in spots
    ]
    match = [
        [
            jnp.where(
                jnp.logical_and(partner[0, 0, 0, k] == s, partner[0, 0, 1, k] == c), 1, 0
            ).astype(jnp.int32)
            for k in range(4)
        ]
        for s, c in spots
    ]

    fetches[0].wait()

    for d in range(4):
        picked = match[d][0] * rows[0, 0, 0:1, :]
        for k in range(1, 4):
            picked = picked + match[d][k] * rows[0, 0, k : k + 1, :]
        node_z[d] = lax.bitwise_and(picked, size_z - 1)
        node_p[d] = lax.shift_right_logical(picked, z_shift)

    def lanes(d, at):
        return pl.ds(pl.multiple_of(d * width + at, 128), CHUNK)

    def over_directions(body):
        lax.fori_loop(0, 4, lambda d, c: (body(d), c)[1], 0)

    def fill_onehot(d):
        for at in range(0, width, CHUNK):
            hit = iota((plane, CHUNK), 0) == node_p[d, :, at : at + CHUNK]
            onehot[:, lanes(d, at)] = jnp.where(hit, 1.0, 0.0).astype(BF)

    def fill_masks(d):
        for at in range(0, width, CHUNK):
            hit = iota((size_z, CHUNK), 0) == node_z[d, :, at : at + CHUNK]
            masks[:, lanes(d, at)] = jnp.where(hit, 1.0, 0.0).astype(BF)

    over_directions(fill_onehot)

    size_bz = classes.shape[4]
    blocks_y = classes.shape[3]
    blocks_x = classes.shape[2]
    for fetch in fetches[1:]:
        fetch.wait()
    el_ref[...] = jnp.zeros_like(el_ref)
    for bx in range(blocks_x):
        ids = classes[0, 0, bx]
        value = jnp.zeros(ids.shape, F32)
        for n in range(coefficients.shape[0]):
            value = jnp.where(ids == n, coefficients[n], value)
        el_ref[bx * blocks_y : (bx + 1) * blocks_y, 0:size_bz] = value
    el_t = el_ref[...].T[:size_bz, : blocks_x * blocks_y]
    plane_at = iota((blocks_x * blocks_y, plane), 1)
    block_at = lax.shift_right_logical(plane_at, y_shift + 2) * blocks_y
    block_at = block_at + lax.shift_right_logical(lax.bitwise_and(plane_at, size_y - 1), 2)
    spread = jnp.where(iota((blocks_x * blocks_y, plane), 0) == block_at, 1.0, 0.0)
    coef_block = exact_dot(el_t, spread)
    spread_z = jnp.where(
        lax.shift_right_logical(iota((size_z, size_bz), 0), 2) == iota((size_z, size_bz), 1), 1.0, 0.0
    )
    root = exact_dot(spread_z, 1.0 / jnp.sqrt(coef_block))
    root_ref[...] = root

    def copy_of(turn, d):
        down, along = d % 2, d // 2
        opposite = d + 1 - 2 * down
        to_sub = lax.rem(me + (1 - along) * (1 + down * (n_sub - 2)), n_sub)
        to_col = lax.rem(col + along * (1 + down * (n_col - 2)), n_col)
        return pltpu.make_async_remote_copy(
            src_ref=send_v.at[turn, d],
            dst_ref=recv_v.at[turn, opposite],
            send_sem=send_sem.at[turn, d],
            recv_sem=recv_sem.at[turn, opposite],
            device_id=(to_sub, to_col),
            device_id_type=MESH,
        )

    def gather(fields):
        stacked = [half for _, field, _ in fields for half in halves(field)]
        stacked = jnp.concatenate(stacked, axis=0)

        def one(d):
            for at in range(0, width, CHUNK):
                part = jnp.dot(
                    stacked,
                    onehot[:, lanes(d, at)],
                    preferred_element_type=F32,
                )
                first = 0
                for turn, field, shift in fields:
                    depth = field.shape[0]
                    both = part[first : first + depth]
                    both = both + part[first + depth : first + 2 * depth]
                    first += 2 * depth
                    at_z = lax.shift_right_logical(node_z[d, :, at : at + CHUNK], shift)
                    hit = iota((depth, CHUNK), 0) == at_z
                    send_v[turn, d, :, at : at + CHUNK] = jnp.sum(
                        jnp.where(hit, both, 0.0), axis=0, keepdims=True
                    )
            for turn, _, _ in fields:
                copy_of(turn, d).start()

        over_directions(one)

    def of_x(i):
        return lax.shift_right_logical(i, y_shift)

    def of_y(i):
        return lax.bitwise_and(i, size_y - 1)

    def expand(mode, of):
        size = mode.shape[0]
        left = jnp.where(of(iota((plane, size), 0)) == iota((plane, size), 1), 1.0, 0.0)
        right = jnp.where(of(iota((size, plane), 1)) == iota((size, plane), 0), 1.0, 0.0)
        left, right = left.astype(BF), right.astype(BF)
        parts = [
            jnp.dot(
                jnp.dot(left, part, preferred_element_type=F32).astype(BF),
                right,
                preferred_element_type=F32,
            )
            for part in halves(mode)
        ]
        return parts[0] + parts[1]

    pair = expand(mode_x[0, 0], of_x) * expand(mode_y[0, 0], of_y)
    side = mode_z[0, 0]
    pair_f[...] = right_operand(pair)
    pair_b[...] = right_operand(pair.T)
    side_f[...] = left_operand(side.T)
    side_b[...] = left_operand(side)

    spectrum = eigen[0]
    modes = spectrum.shape[1]
    mode_at = iota((modes, plane), 0)
    to_plane = jnp.logical_or(
        mode_at == of_x(iota((modes, plane), 1)),
        mode_at == size_x + of_y(iota((modes, plane), 1)),
    )
    plane_eigen = exact_dot(
        jnp.broadcast_to(spectrum, (8, modes)), jnp.where(to_plane, 1.0, 0.0)
    )[0:1]
    z_at = iota((size_z, modes), 0) + size_x + size_y == iota((size_z, modes), 1)
    z_eigen = jnp.sum(jnp.where(z_at, spectrum, 0.0), axis=1, keepdims=True)
    lam_ref[...] = 1.0 / (z_eigen + plane_eigen)

    def forward(field):
        mixed = times(field * root_ref[...], pair_f[...])
        return jnp.dot(side_f[...], right_operand(mixed), preferred_element_type=F32)

    def backward(spectral):
        mixed = times(spectral, pair_b[...])
        return root_ref[...] * jnp.dot(
            side_b[...], right_operand(mixed), preferred_element_type=F32
        )

    load_field = backward(lam_ref[...] * forward(loads[0, 0].reshape(plane, size_z).T))
    pl.semaphore_wait(barrier, n_all - 1 if direct else n_sub - 1 + n_col - 1)

    def cinv_copy(s):
        return pltpu.make_async_remote_copy(
            src_ref=cinv,
            dst_ref=cfull.at[col],
            send_sem=cinv_send.at[s],
            recv_sem=cinv_recv.at[s],
            device_id=(me, lax.rem(col + s, n_col)),
            device_id_type=MESH,
        )

    each(1, n_col, lambda s: cinv_copy(s).start())
    cfull[col] = cinv[...]
    gather([(0, coef_block, 2), (1, load_field, 0)])
    over_directions(fill_masks)

    lane_z = iota((corners, size_z), 1)
    lane_p = iota((corners, plane), 1)
    lane_n = iota((corners, padded), 1)
    at_z = jnp.zeros((corners, size_z), jnp.int32)
    at_p = jnp.zeros((corners, plane), jnp.int32)
    at_n = jnp.zeros((corners, padded), jnp.int32)
    for t in range(corners):
        node = corner_row[0, 0, t]
        at_z = jnp.where(iota((corners, size_z), 0) == t, node, at_z)
        at_p = jnp.where(iota((corners, plane), 0) == t, node, at_p)
        at_n = jnp.where(iota((corners, padded), 0) == t, corner_id[0, 0, t], at_n)
    pick_z = jnp.where(lax.bitwise_and(at_z, size_z - 1) == lane_z, 1.0, 0.0)
    pick_p = jnp.where(lax.shift_right_logical(at_p, z_shift) == lane_p, 1.0, 0.0)
    pick_n = jnp.where(at_n == lane_n, 1.0, 0.0)
    corner_root = jnp.sum(exact_dot(pick_z, root) * pick_p, axis=1, keepdims=True)
    corner_z = exact_dot(pick_z, side)
    corner_p = exact_dot(pick_p, pair) * corner_root
    high, low = halves(corner_z)
    pad_ref[...] = jnp.zeros_like(pad_ref)
    pad_ref[0:corners, :] = high.astype(F32)
    pad_ref[corners : 2 * corners, :] = high.astype(F32)
    pad_ref[2 * corners : 3 * corners, :] = low.astype(F32)
    corner_l[...] = pad_ref[...].T.astype(BF)
    corner_z3 = jnp.concatenate([high.astype(F32), high.astype(F32), low.astype(F32)], axis=1)
    corner_z3 = corner_z3.astype(BF)

    def sum_copies(turn):
        count = n_all if direct else n_sub

        def copy(s):
            return pltpu.make_async_remote_copy(
                src_ref=vec_sub.at[turn, 0],
                dst_ref=vec_sub.at[turn, s],
                send_sem=sub_send.at[turn, s],
                recv_sem=sub_recv.at[turn, s],
                device_id=other(s) if direct else (lax.rem(me + s, n_sub), col),
                device_id_type=MESH,
            )

        return count, copy

    def sum_start(turn, vector):
        vec_sub[turn, 0] = vector
        count, copy = sum_copies(turn)
        each(1, count, lambda s: copy(s).start())

    def sum_finish(turn):
        count, copy = sum_copies(turn)
        each(1, count, lambda s: copy(s).wait())
        mine = jnp.sum(vec_sub[turn], axis=0)
        if direct:
            return mine
        mine_col[turn] = mine

        def col_copy(s):
            return pltpu.make_async_remote_copy(
                src_ref=mine_col.at[turn],
                dst_ref=vec_col.at[turn, s],
                send_sem=col_send.at[turn, s],
                recv_sem=col_recv.at[turn, s],
                device_id=(me, lax.rem(col + s, n_col)),
                device_id_type=MESH,
            )

        each(1, n_col, lambda s: col_copy(s).start())
        vec_col[turn, 0] = mine
        each(1, n_col, lambda s: col_copy(s).wait())
        return jnp.sum(vec_col[turn], axis=0)

    def jump(turn, d):
        copy_of(turn, d ^ 1).wait_recv()
        return signs[d] * (send_v[turn, d] - recv_v[turn, d])

    def scatter(value_of):
        total = jnp.zeros((2 * size_z, plane), F32)
        for d in range(4):
            high, low = halves(signs[d] * value_of(d))
            for at in range(0, width, CHUNK):
                here = slice(at, at + CHUNK)
                mask = masks[:, d * width + at : d * width + at + CHUNK]
                placed_rows[d, :size_z, here] = mask * high[:, here]
                placed_rows[d, size_z:, here] = mask * low[:, here]
            total = total + lax.dot_general(
                placed_rows[d],
                onehot[:, d * width : (d + 1) * width],
                (((1,), (1,)), ((), ())),
                preferred_element_type=F32,
            )
        return total[:size_z] + total[size_z:]

    def all_of(x):
        return jnp.sum(jnp.sum(x, axis=0, keepdims=True), axis=1, keepdims=True)

    def dot4(a, b):
        total = a[0] * b[0]
        for d in range(1, 4):
            total = total + a[d] * b[d]
        return jnp.sum(total, axis=1, keepdims=True)

    lane = iota((1, padded), 1)

    def apply(turn, value_of, scalars_of):
        modal = forward(scatter(value_of))
        scalars = scalars_of()
        spectral = lam_ref[...] * modal
        energy = all_of(modal * spectral)
        at_corner = jnp.sum(
            jnp.dot(corner_z3, right_operand(spectral), preferred_element_type=F32) * corner_p,
            axis=1,
            keepdims=True,
        )
        vector = jnp.sum(pick_n * at_corner, axis=0, keepdims=True)
        for n, scalar in enumerate([energy] + scalars):
            vector = jnp.where(lane == total_corners + n, scalar, vector)
        sum_start(turn - 2, vector)
        if turn == 2:
            each(1, n_col, lambda s: cinv_copy(s).wait())
            inverse = cfull[...].reshape(total_corners, total_corners)
            own_rows[...] = exact_dot(pick_n[:, :total_corners], inverse)
        total = sum_finish(turn - 2)
        at_corners = total[:, :total_corners]
        local = jnp.sum(own_rows[...] * at_corners, axis=1, keepdims=True)
        high, low = halves(corner_p * local)
        high, low = high.astype(F32), low.astype(F32)
        rest = jnp.zeros((size_z - 3 * corners, plane), F32)
        source = jnp.concatenate([high, low, high, rest], axis=0).astype(BF)
        extra = jnp.dot(corner_l[...], source, preferred_element_type=F32)
        gather([(turn, backward(spectral + lam_ref[...] * extra), 0)])
        inverse = cfull[...].reshape(total_corners, total_corners)
        coarse = exact_dot(jnp.broadcast_to(at_corners, (8, total_corners)), inverse)[0:1]
        quad = jnp.sum(at_corners * coarse, axis=1, keepdims=True)
        got = [
            jnp.sum(jnp.where(lane == total_corners + n, total, 0.0), axis=1, keepdims=True)
            for n in range(1 + len(scalars))
        ]
        return 2.0 * (got[0] + quad), got[1:]

    four = range(4)
    weight, resid, direction, image = [None] * 4, [None] * 4, [None] * 4, [None] * 4

    def first_value(d):
        copy_of(0, d ^ 1).wait_recv()
        near, far = send_v[0, d], recv_v[0, d]
        weight[d] = near * far / (near + far)
        resid[d] = jump(1, d)
        direction[d] = weight[d] * resid[d]
        return direction[d]

    image_dot, (rz,) = apply(2, first_value, lambda: [dot4(resid, direction)])
    alpha = rz / image_dot
    beta = None
    mult = [alpha * direction[d] for d in four]

    def image_at(turn, d):
        fresh = jump(turn, d)
        return fresh if beta is None else fresh + beta * image[d]

    for step in range(1, ITERS):
        precond = [None] * 4

        def next_value(d):
            image[d] = image_at(1 + step, d)
            resid[d] = resid[d] - alpha * image[d]
            precond[d] = weight[d] * resid[d]
            return precond[d]

        own_dot, (rz_next, cross) = apply(
            2 + step, next_value, lambda: [dot4(resid, precond), dot4(precond, image)]
        )
        beta = rz_next / rz
        image_dot = own_dot + 2.0 * beta * cross + beta * beta * image_dot
        alpha = rz_next / image_dot
        rz = rz_next
        direction = [precond[d] + beta * direction[d] for d in four]
        mult = [mult[d] + alpha * direction[d] for d in four]
    image = [image_at(1 + ITERS, d) for d in four]
    resid = [resid[d] - alpha * image[d] for d in four]
    for k in range(4):
        share = [match[d][k].astype(F32) for d in four]
        one = share[0] * mult[0]
        two = share[0] * resid[0]
        for d in range(1, 4):
            one = one + share[d] * mult[d]
            two = two + share[d] * resid[d]
        out_mult[0, 0, k : k + 1, :] = one
        out_resid[0, 0, k : k + 1, :] = two
    for turn in range(2 + ITERS):
        for d in four:
            copy_of(turn, d).wait_send()


def on_device(n_sub, n_col, *args):
    args = list(args)
    args[7] = jnp.swapaxes(args[7], 2, 3)
    loads, mode_x, mode_y, mode_z, eigen, classes = args[:6]
    rows, cinv = args[8], args[11]
    size_z = mode_z.shape[2]
    plane = mode_x.shape[2] * mode_y.shape[2]
    width = rows.shape[3]
    corners = args[10].shape[2]
    total_corners = cinv.shape[1]
    padded = -(-(total_corners + 3) // 128) * 128
    turns = 2 + ITERS
    first = n_sub * n_col if n_sub * n_col <= DIRECT else n_sub
    vmem = pl.BlockSpec(memory_space=pltpu.VMEM)
    hbm = pl.BlockSpec(memory_space=pltpu.HBM)
    smem = pl.BlockSpec(memory_space=pltpu.SMEM)
    dma = pltpu.SemaphoreType.DMA
    out = jax.ShapeDtypeStruct(rows.shape, F32)
    return pl.pallas_call(
        functools.partial(kernel, n_sub, n_col),
        out_shape=(out, out),
        in_specs=[hbm] * 6 + [smem] * 2 + [hbm] + [smem] * 2 + [hbm],
        out_specs=(vmem, vmem),
        scratch_shapes=[
            *[
                pltpu.VMEM(x.shape, x.dtype)
                for x in (loads, mode_x, mode_y, mode_z, eigen, classes, rows, cinv)
            ],
            dma((8,)),
            pltpu.VMEM((plane, 4 * width), BF),
            pltpu.VMEM((size_z, 4 * width), BF),
            pltpu.VMEM((4, 2 * size_z, width), BF),
            pltpu.VMEM((4, 1, width), jnp.int32),
            pltpu.VMEM((4, 1, width), jnp.int32),
            pltpu.VMEM((128, 128), F32),
            pltpu.VMEM((3 * plane, plane), BF),
            pltpu.VMEM((3 * plane, plane), BF),
            pltpu.VMEM((size_z, 3 * size_z), BF),
            pltpu.VMEM((size_z, 3 * size_z), BF),
            pltpu.VMEM((size_z, plane), F32),
            pltpu.VMEM((size_z, plane), F32),
            pltpu.VMEM((size_z, size_z), BF),
            pltpu.VMEM((size_z, size_z), F32),
            pltpu.VMEM((n_col,) + cinv.shape, F32),
            pltpu.VMEM((corners, total_corners), F32),
            pltpu.VMEM((turns, 4, 1, width), F32),
            pltpu.VMEM((turns, 4, 1, width), F32),
            pltpu.VMEM((ITERS, first, 1, padded), F32),
            pltpu.VMEM((ITERS, n_col, 1, padded), F32),
            pltpu.VMEM((ITERS, 1, padded), F32),
            dma((turns, 4)),
            dma((turns, 4)),
            dma((ITERS, first)),
            dma((ITERS, first)),
            dma((ITERS, n_col)),
            dma((ITERS, n_col)),
            dma((n_col,)),
            dma((n_col,)),
        ],
        compiler_params=pltpu.CompilerParams(
            collective_id=0, has_side_effects=True, vmem_limit_bytes=60 * 1024 * 1024
        ),
        name="feti_pcg",
    )(*args)


def solution(mesh):
    placed = (
        P("sub", "coarse", None, None, None),
        P("sub", "coarse", None, None),
        P("sub", "coarse", None, None),
        P("sub", "coarse", None, None),
        P("sub", "coarse", None),
        P("sub", "coarse", None, None, None),
        P(),
        P("sub", "coarse", None, None),
        P("sub", "coarse", None, None),
        P("sub", "coarse", None),
        P("sub", "coarse", None),
        P("coarse", None),
    )
    return jax.shard_map(
        functools.partial(on_device, mesh.shape["sub"], mesh.shape["coarse"]),
        mesh=mesh,
        in_specs=placed,
        out_specs=(P("sub", "coarse", None, None), P("sub", "coarse", None, None)),
        check_vma=False,
    )
```

```python
import functools

import jax
import jax.numpy as jnp
from jax import lax
from jax.experimental import pallas as pl
from jax.experimental.pallas import tpu as pltpu
from jax.sharding import PartitionSpec as P

ITERS = 2
CHUNK = 256
DIRECT = 64
BF = jnp.bfloat16
F32 = jnp.float32
HI = lax.Precision.HIGHEST
MESH = pl.DeviceIdType.MESH


def exact_dot(a, b):
    return jnp.dot(a, b, precision=HI, preferred_element_type=F32)


def halves(x):
    high = x.astype(BF)
    return high, (x - high.astype(F32)).astype(BF)


def iota(shape, dim):
    return lax.broadcasted_iota(jnp.int32, shape, dim)


def each(low, high, body):
    if high - low <= 8:
        for i in range(low, high):
            body(i)
    else:
        lax.fori_loop(low, high, lambda i, c: (body(i), c)[1], 0)


def right_operand(x):
    high, low = halves(x)
    return jnp.concatenate([high, low, high], axis=0)


def left_operand(x):
    high, low = halves(x)
    return jnp.concatenate([high, high, low], axis=1)


def times(x, right):
    return jnp.dot(left_operand(x), right, preferred_element_type=F32)


def kernel(
    n_sub,
    n_col,
    loads_hbm,
    mode_x_hbm,
    mode_y_hbm,
    mode_z_hbm,
    eigen_hbm,
    classes_hbm,
    coefficients,
    partner,
    rows_hbm,
    corner_id,
    corner_row,
    cinv_hbm,
    out_mult,
    out_resid,
    loads,
    mode_x,
    mode_y,
    mode_z,
    eigen,
    classes,
    rows,
    cinv,
    load_sem,
    onehot,
    masks,
    placed_rows,
    node_z,
    node_p,
    el_ref,
    pair_f,
    pair_b,
    side_f,
    side_b,
    lam_ref,
    root_ref,
    corner_l,
    pad_ref,
    cfull,
    own_rows,
    send_v,
    recv_v,
    vec_sub,
    vec_col,
    mine_col,
    send_sem,
    recv_sem,
    sub_send,
    sub_recv,
    col_send,
    col_recv,
    cinv_send,
    cinv_recv,
):
    me = lax.axis_index("sub")
    col = lax.axis_index("coarse")
    size_x = mode_x.shape[2]
    size_y = mode_y.shape[2]
    size_z = mode_z.shape[2]
    plane = size_x * size_y
    width = rows.shape[3]
    corners = corner_row.shape[2]
    total_corners = cinv.shape[1]
    padded = vec_sub.shape[3]
    z_shift = size_z.bit_length() - 1
    y_shift = size_y.bit_length() - 1
    assert size_z == 1 << z_shift and size_y == 1 << y_shift

    fetches = [
        pltpu.make_async_copy(source, target, load_sem.at[n])
        for n, (source, target) in enumerate(
            (
                (rows_hbm, rows),
                (classes_hbm, classes),
                (cinv_hbm, cinv),
                (mode_x_hbm, mode_x),
                (mode_y_hbm, mode_y),
                (mode_z_hbm, mode_z),
                (eigen_hbm, eigen),
                (loads_hbm, loads),
            )
        )
    ]
    for fetch in fetches:
        fetch.start()
    barrier = pltpu.get_barrier_semaphore()

    def greet_sub(s):
        pl.semaphore_signal(
            barrier, inc=1, device_id=(lax.rem(me + s, n_sub), col), device_id_type=MESH
        )

    def greet_col(s):
        pl.semaphore_signal(
            barrier, inc=1, device_id=(me, lax.rem(col + s, n_col)), device_id_type=MESH
        )

    n_all = n_sub * n_col
    direct = n_all <= DIRECT
    own = me * n_col + col

    def other(s):
        flat = lax.rem(own + s, n_all)
        return lax.div(flat, n_col), lax.rem(flat, n_col)

    def greet_all(s):
        pl.semaphore_signal(barrier, inc=1, device_id=other(s), device_id_type=MESH)

    if direct:
        each(1, n_all, greet_all)
    else:
        each(1, n_sub, greet_sub)
        each(1, n_col, greet_col)

    spots = (
        (lax.rem(me + 1, n_sub), col),
        (lax.rem(me + n_sub - 1, n_sub), col),
        (me, lax.rem(col + 1, n_col)),
        (me, lax.rem(col + n_col - 1, n_col)),
    )
    signs = [
        jnp.where(me * n_col + col < s * n_col + c, 1.0, -1.0).astype(F32) for s, c in spots
    ]
    match = [
        [
            jnp.where(
                jnp.logical_and(partner[0, 0, 0, k] == s, partner[0, 0, 1, k] == c), 1, 0
            ).astype(jnp.int32)
            for k in range(4)
        ]
        for s, c in spots
    ]

    fetches[0].wait()

    for d in range(4):
        picked = match[d][0] * rows[0, 0, 0:1, :]
        for k in range(1, 4):
            picked = picked + match[d][k] * rows[0, 0, k : k + 1, :]
        node_z[d] = lax.bitwise_and(picked, size_z - 1)
        node_p[d] = lax.shift_right_logical(picked, z_shift)

    def lanes(d, at):
        return pl.ds(pl.multiple_of(d * width + at, 128), CHUNK)

    def over_directions(body):
        lax.fori_loop(0, 4, lambda d, c: (body(d), c)[1], 0)

    def fill_onehot(d):
        for at in range(0, width, CHUNK):
            hit = iota((plane, CHUNK), 0) == node_p[d, :, at : at + CHUNK]
            onehot[:, lanes(d, at)] = jnp.where(hit, 1.0, 0.0).astype(BF)

    def fill_masks(d):
        for at in range(0, width, CHUNK):
            hit = iota((size_z, CHUNK), 0) == node_z[d, :, at : at + CHUNK]
            masks[:, lanes(d, at)] = jnp.where(hit, 1.0, 0.0).astype(BF)

    over_directions(fill_onehot)

    size_bz = classes.shape[4]
    blocks_y = classes.shape[3]
    blocks_x = classes.shape[2]
    for fetch in fetches[1:]:
        fetch.wait()
    el_ref[...] = jnp.zeros_like(el_ref)
    for bx in range(blocks_x):
        ids = classes[0, 0, bx]
        value = jnp.zeros(ids.shape, F32)
        for n in range(coefficients.shape[0]):
            value = jnp.where(ids == n, coefficients[n], value)
        el_ref[bx * blocks_y : (bx + 1) * blocks_y, 0:size_bz] = value
    el_t = el_ref[...].T[:size_bz, : blocks_x * blocks_y]
    plane_at = iota((blocks_x * blocks_y, plane), 1)
    block_at = lax.shift_right_logical(plane_at, y_shift + 2) * blocks_y
    block_at = block_at + lax.shift_right_logical(lax.bitwise_and(plane_at, size_y - 1), 2)
    spread = jnp.where(iota((blocks_x * blocks_y, plane), 0) == block_at, 1.0, 0.0)
    coef_block = exact_dot(el_t, spread)
    spread_z = jnp.where(
        lax.shift_right_logical(iota((size_z, size_bz), 0), 2) == iota((size_z, size_bz), 1), 1.0, 0.0
    )
    root = exact_dot(spread_z, 1.0 / jnp.sqrt(coef_block))
    root_ref[...] = root

    def copy_of(turn, d):
        down, along = d % 2, d // 2
        opposite = d + 1 - 2 * down
        to_sub = lax.rem(me + (1 - along) * (1 + down * (n_sub - 2)), n_sub)
        to_col = lax.rem(col + along * (1 + down * (n_col - 2)), n_col)
        return pltpu.make_async_remote_copy(
            src_ref=send_v.at[turn, d],
            dst_ref=recv_v.at[turn, opposite],
            send_sem=send_sem.at[turn, d],
            recv_sem=recv_sem.at[turn, opposite],
            device_id=(to_sub, to_col),
            device_id_type=MESH,
        )

    def gather(fields):
        stacked = [half for _, field, _ in fields for half in halves(field)]
        stacked = jnp.concatenate(stacked, axis=0)

        def one(d):
            for at in range(0, width, CHUNK):
                part = jnp.dot(
                    stacked,
                    onehot[:, lanes(d, at)],
                    preferred_element_type=F32,
                )
                first = 0
                for turn, field, shift in fields:
                    depth = field.shape[0]
                    both = part[first : first + depth]
                    both = both + part[first + depth : first + 2 * depth]
                    first += 2 * depth
                    at_z = lax.shift_right_logical(node_z[d, :, at : at + CHUNK], shift)
                    hit = iota((depth, CHUNK), 0) == at_z
                    send_v[turn, d, :, at : at + CHUNK] = jnp.sum(
                        jnp.where(hit, both, 0.0), axis=0, keepdims=True
                    )
            for turn, _, _ in fields:
                copy_of(turn, d).start()

        over_directions(one)

    def of_x(i):
        return lax.shift_right_logical(i, y_shift)

    def of_y(i):
        return lax.bitwise_and(i, size_y - 1)

    def expand(mode, of):
        size = mode.shape[0]
        left = jnp.where(of(iota((plane, size), 0)) == iota((plane, size), 1), 1.0, 0.0)
        right = jnp.where(of(iota((size, plane), 1)) == iota((size, plane), 0), 1.0, 0.0)
        left, right = left.astype(BF), right.astype(BF)
        parts = [
            jnp.dot(
                jnp.dot(left, part, preferred_element_type=F32).astype(BF),
                right,
                preferred_element_type=F32,
            )
            for part in halves(mode)
        ]
        return parts[0] + parts[1]

    pair = expand(mode_x[0, 0], of_x) * expand(mode_y[0, 0], of_y)
    side = mode_z[0, 0]
    pair_f[...] = right_operand(pair)
    pair_b[...] = right_operand(pair.T)
    side_f[...] = left_operand(side.T)
    side_b[...] = left_operand(side)

    spectrum = eigen[0]
    modes = spectrum.shape[1]
    mode_at = iota((modes, plane), 0)
    to_plane = jnp.logical_or(
        mode_at == of_x(iota((modes, plane), 1)),
        mode_at == size_x + of_y(iota((modes, plane), 1)),
    )
    plane_eigen = exact_dot(
        jnp.broadcast_to(spectrum, (8, modes)), jnp.where(to_plane, 1.0, 0.0)
    )[0:1]
    z_at = iota((size_z, modes), 0) + size_x + size_y == iota((size_z, modes), 1)
    z_eigen = jnp.sum(jnp.where(z_at, spectrum, 0.0), axis=1, keepdims=True)
    lam_ref[...] = 1.0 / (z_eigen + plane_eigen)

    def forward(field):
        mixed = times(field * root_ref[...], pair_f[...])
        return jnp.dot(side_f[...], right_operand(mixed), preferred_element_type=F32)

    def backward(spectral):
        mixed = times(spectral, pair_b[...])
        return root_ref[...] * jnp.dot(
            side_b[...], right_operand(mixed), preferred_element_type=F32
        )

    load_field = backward(lam_ref[...] * forward(loads[0, 0].reshape(plane, size_z).T))
    pl.semaphore_wait(barrier, n_all - 1 if direct else n_sub - 1 + n_col - 1)

    def cinv_copy(s):
        return pltpu.make_async_remote_copy(
            src_ref=cinv,
            dst_ref=cfull.at[col],
            send_sem=cinv_send.at[s],
            recv_sem=cinv_recv.at[s],
            device_id=(me, lax.rem(col + s, n_col)),
            device_id_type=MESH,
        )

    each(1, n_col, lambda s: cinv_copy(s).start())
    cfull[col] = cinv[...]
    gather([(0, coef_block, 2), (1, load_field, 0)])
    over_directions(fill_masks)

    lane_z = iota((corners, size_z), 1)
    lane_p = iota((corners, plane), 1)
    lane_n = iota((corners, padded), 1)
    at_z = jnp.zeros((corners, size_z), jnp.int32)
    at_p = jnp.zeros((corners, plane), jnp.int32)
    at_n = jnp.zeros((corners, padded), jnp.int32)
    for t in range(corners):
        node = corner_row[0, 0, t]
        at_z = jnp.where(iota((corners, size_z), 0) == t, node, at_z)
        at_p = jnp.where(iota((corners, plane), 0) == t, node, at_p)
        at_n = jnp.where(iota((corners, padded), 0) == t, corner_id[0, 0, t], at_n)
    pick_z = jnp.where(lax.bitwise_and(at_z, size_z - 1) == lane_z, 1.0, 0.0)
    pick_p = jnp.where(lax.shift_right_logical(at_p, z_shift) == lane_p, 1.0, 0.0)
    pick_n = jnp.where(at_n == lane_n, 1.0, 0.0)
    corner_root = jnp.sum(exact_dot(pick_z, root) * pick_p, axis=1, keepdims=True)
    corner_z = exact_dot(pick_z, side)
    corner_p = exact_dot(pick_p, pair) * corner_root
    high, low = halves(corner_z)
    pad_ref[...] = jnp.zeros_like(pad_ref)
    pad_ref[0:corners, :] = high.astype(F32)
    pad_ref[corners : 2 * corners, :] = high.astype(F32)
    pad_ref[2 * corners : 3 * corners, :] = low.astype(F32)
    corner_l[...] = pad_ref[...].T.astype(BF)
    corner_z3 = jnp.concatenate([high.astype(F32), high.astype(F32), low.astype(F32)], axis=1)
    corner_z3 = corner_z3.astype(BF)

    def sum_copies(turn):
        count = n_all if direct else n_sub

        def copy(s):
            return pltpu.make_async_remote_copy(
                src_ref=vec_sub.at[turn, 0],
                dst_ref=vec_sub.at[turn, s],
                send_sem=sub_send.at[turn, s],
                recv_sem=sub_recv.at[turn, s],
                device_id=other(s) if direct else (lax.rem(me + s, n_sub), col),
                device_id_type=MESH,
            )

        return count, copy

    def sum_start(turn, vector):
        vec_sub[turn, 0] = vector
        count, copy = sum_copies(turn)
        each(1, count, lambda s: copy(s).start())

    def sum_finish(turn):
        count, copy = sum_copies(turn)
        each(1, count, lambda s: copy(s).wait())
        mine = jnp.sum(vec_sub[turn], axis=0)
        if direct:
            return mine
        mine_col[turn] = mine

        def col_copy(s):
            return pltpu.make_async_remote_copy(
                src_ref=mine_col.at[turn],
                dst_ref=vec_col.at[turn, s],
                send_sem=col_send.at[turn, s],
                recv_sem=col_recv.at[turn, s],
                device_id=(me, lax.rem(col + s, n_col)),
                device_id_type=MESH,
            )

        each(1, n_col, lambda s: col_copy(s).start())
        vec_col[turn, 0] = mine
        each(1, n_col, lambda s: col_copy(s).wait())
        return jnp.sum(vec_col[turn], axis=0)

    def jump(turn, d):
        copy_of(turn, d ^ 1).wait_recv()
        return signs[d] * (send_v[turn, d] - recv_v[turn, d])

    def scatter(value_of):
        total = jnp.zeros((2 * size_z, plane), F32)
        for d in range(4):
            high, low = halves(signs[d] * value_of(d))
            for at in range(0, width, CHUNK):
                here = slice(at, at + CHUNK)
                mask = masks[:, d * width + at : d * width + at + CHUNK]
                placed_rows[d, :size_z, here] = mask * high[:, here]
                placed_rows[d, size_z:, here] = mask * low[:, here]
            total = total + lax.dot_general(
                placed_rows[d],
                onehot[:, d * width : (d + 1) * width],
                (((1,), (1,)), ((), ())),
                preferred_element_type=F32,
            )
        return total[:size_z] + total[size_z:]

    def all_of(x):
        return jnp.sum(jnp.sum(x, axis=0, keepdims=True), axis=1, keepdims=True)

    def dot4(a, b):
        total = a[0] * b[0]
        for d in range(1, 4):
            total = total + a[d] * b[d]
        return jnp.sum(total, axis=1, keepdims=True)

    lane = iota((1, padded), 1)

    def apply(turn, value_of, scalars_of):
        modal = forward(scatter(value_of))
        scalars = scalars_of()
        spectral = lam_ref[...] * modal
        energy = all_of(modal * spectral)
        at_corner = jnp.sum(
            jnp.dot(corner_z3, right_operand(spectral), preferred_element_type=F32) * corner_p,
            axis=1,
            keepdims=True,
        )
        vector = jnp.sum(pick_n * at_corner, axis=0, keepdims=True)
        for n, scalar in enumerate([energy] + scalars):
            vector = jnp.where(lane == total_corners + n, scalar, vector)
        sum_start(turn - 2, vector)
        if turn == 2:
            each(1, n_col, lambda s: cinv_copy(s).wait())
            inverse = cfull[...].reshape(total_corners, total_corners)
            own_rows[...] = exact_dot(pick_n[:, :total_corners], inverse)
        total = sum_finish(turn - 2)
        at_corners = total[:, :total_corners]
        local = jnp.sum(own_rows[...] * at_corners, axis=1, keepdims=True)
        high, low = halves(corner_p * local)
        high, low = high.astype(F32), low.astype(F32)
        rest = jnp.zeros((size_z - 3 * corners, plane), F32)
        source = jnp.concatenate([high, low, high, rest], axis=0).astype(BF)
        extra = jnp.dot(corner_l[...], source, preferred_element_type=F32)
        gather([(turn, backward(spectral + lam_ref[...] * extra), 0)])
        inverse = cfull[...].reshape(total_corners, total_corners)
        coarse = exact_dot(jnp.broadcast_to(at_corners, (8, total_corners)), inverse)[0:1]
        quad = jnp.sum(at_corners * coarse, axis=1, keepdims=True)
        got = [
            jnp.sum(jnp.where(lane == total_corners + n, total, 0.0), axis=1, keepdims=True)
            for n in range(1 + len(scalars))
        ]
        return 2.0 * (got[0] + quad), got[1:]

    four = range(4)
    weight, resid, direction, image = [None] * 4, [None] * 4, [None] * 4, [None] * 4

    def first_value(d):
        copy_of(0, d ^ 1).wait_recv()
        near, far = send_v[0, d], recv_v[0, d]
        weight[d] = near * far / (near + far)
        resid[d] = jump(1, d)
        direction[d] = weight[d] * resid[d]
        return direction[d]

    image_dot, (rz,) = apply(2, first_value, lambda: [dot4(resid, direction)])
    alpha = rz / image_dot
    beta = None
    mult = [alpha * direction[d] for d in four]

    def image_at(turn, d):
        fresh = jump(turn, d)
        return fresh if beta is None else fresh + beta * image[d]

    for step in range(1, ITERS):
        precond = [None] * 4

        def next_value(d):
            image[d] = image_at(1 + step, d)
            resid[d] = resid[d] - alpha * image[d]
            precond[d] = weight[d] * resid[d]
            return precond[d]

        own_dot, (rz_next, cross) = apply(
            2 + step, next_value, lambda: [dot4(resid, precond), dot4(precond, image)]
        )
        beta = rz_next / rz
        image_dot = own_dot + 2.0 * beta * cross + beta * beta * image_dot
        alpha = rz_next / image_dot
        rz = rz_next
        direction = [precond[d] + beta * direction[d] for d in four]
        mult = [mult[d] + alpha * direction[d] for d in four]
    image = [image_at(1 + ITERS, d) for d in four]
    resid = [resid[d] - alpha * image[d] for d in four]
    for k in range(4):
        share = [match[d][k].astype(F32) for d in four]
        one = share[0] * mult[0]
        two = share[0] * resid[0]
        for d in range(1, 4):
            one = one + share[d] * mult[d]
            two = two + share[d] * resid[d]
        out_mult[0, 0, k : k + 1, :] = one
        out_resid[0, 0, k : k + 1, :] = two
    for turn in range(2 + ITERS):
        for d in four:
            copy_of(turn, d).wait_send()


def on_device(n_sub, n_col, *args):
    args = list(args)
    args[7] = jnp.swapaxes(args[7], 2, 3)
    loads, mode_x, mode_y, mode_z, eigen, classes = args[:6]
    rows, cinv = args[8], args[11]
    size_z = mode_z.shape[2]
    plane = mode_x.shape[2] * mode_y.shape[2]
    width = rows.shape[3]
    corners = args[10].shape[2]
    total_corners = cinv.shape[1]
    padded = -(-(total_corners + 3) // 128) * 128
    turns = 2 + ITERS
    first = n_sub * n_col if n_sub * n_col <= DIRECT else n_sub
    vmem = pl.BlockSpec(memory_space=pltpu.VMEM)
    hbm = pl.BlockSpec(memory_space=pltpu.HBM)
    smem = pl.BlockSpec(memory_space=pltpu.SMEM)
    dma = pltpu.SemaphoreType.DMA
    out = jax.ShapeDtypeStruct(rows.shape, F32)
    return pl.pallas_call(
        functools.partial(kernel, n_sub, n_col),
        out_shape=(out, out),
        in_specs=[hbm] * 6 + [smem] * 2 + [hbm] + [smem] * 2 + [hbm],
        out_specs=(vmem, vmem),
        scratch_shapes=[
            *[
                pltpu.VMEM(x.shape, x.dtype)
                for x in (loads, mode_x, mode_y, mode_z, eigen, classes, rows, cinv)
            ],
            dma((8,)),
            pltpu.VMEM((plane, 4 * width), BF),
            pltpu.VMEM((size_z, 4 * width), BF),
            pltpu.VMEM((4, 2 * size_z, width), BF),
            pltpu.VMEM((4, 1, width), jnp.int32),
            pltpu.VMEM((4, 1, width), jnp.int32),
            pltpu.VMEM((128, 128), F32),
            pltpu.VMEM((3 * plane, plane), BF),
            pltpu.VMEM((3 * plane, plane), BF),
            pltpu.VMEM((size_z, 3 * size_z), BF),
            pltpu.VMEM((size_z, 3 * size_z), BF),
            pltpu.VMEM((size_z, plane), F32),
            pltpu.VMEM((size_z, plane), F32),
            pltpu.VMEM((size_z, size_z), BF),
            pltpu.VMEM((size_z, size_z), F32),
            pltpu.VMEM((n_col,) + cinv.shape, F32),
            pltpu.VMEM((corners, total_corners), F32),
            pltpu.VMEM((turns, 4, 1, width), F32),
            pltpu.VMEM((turns, 4, 1, width), F32),
            pltpu.VMEM((ITERS, first, 1, padded), F32),
            pltpu.VMEM((ITERS, n_col, 1, padded), F32),
            pltpu.VMEM((ITERS, 1, padded), F32),
            dma((turns, 4)),
            dma((turns, 4)),
            dma((ITERS, first)),
            dma((ITERS, first)),
            dma((ITERS, n_col)),
            dma((ITERS, n_col)),
            dma((n_col,)),
            dma((n_col,)),
        ],
        compiler_params=pltpu.CompilerParams(
            collective_id=0, has_side_effects=True, vmem_limit_bytes=60 * 1024 * 1024
        ),
        name="feti_pcg",
    )(*args)


def solution(mesh):
    placed = (
        P("sub", "coarse", None, None, None),
        P("sub", "coarse", None, None),
        P("sub", "coarse", None, None),
        P("sub", "coarse", None, None),
        P("sub", "coarse", None),
        P("sub", "coarse", None, None, None),
        P(),
        P("sub", "coarse", None, None),
        P("sub", "coarse", None, None),
        P("sub", "coarse", None),
        P("sub", "coarse", None),
        P("coarse", None),
    )
    return jax.shard_map(
        functools.partial(on_device, mesh.shape["sub"], mesh.shape["coarse"]),
        mesh=mesh,
        in_specs=placed,
        out_specs=(P("sub", "coarse", None, None), P("sub", "coarse", None, None)),
        check_vma=False,
    )
```
